32 devices in a mesh: dp: 4 (over x, core), tm: 8 (over z, y).
Axes of the slice: x: 2, y: 2, z: 4, core: 2. Of those that a mesh axis runs over, the one named last changes fastest.
Arguments:
- clips: bfloat16 [4, 16, 512, 1152], P('dp', 'tm'), may hold values from -6 to 6
- w_space_qkv: bfloat16 [1152, 3456], P('dp'), may hold values from -0.1875 to 0.1875
- w_space_out: bfloat16 [1152, 1152], P('dp'), may hold values from -1 to 1
- w_time_qkv: bfloat16 [1152, 3456], P('dp'), may hold values from -0.1875 to 0.1875
- w_time_out: bfloat16 [1152, 1152], P('dp'), may hold values from -1 to 1
- space_pattern: int32 [8, 4], replicated, may hold values from 0 to 7, as said below
- time_pattern: int32 [8, 4], replicated, may hold values from 0 to 7, as said below
Outputs:
- layer_out: bfloat16 [4, 16, 512, 1152], P('dp', 'tm')
The draws below stay inside these ranges and needn't reach their ends.
Inputs may be any that keep to these rules, and one draw needn't show every extreme that they name: `space_pattern`: row i starts with i; the other entries are any blocks, repeats allowed. `time_pattern`: row i starts with i; every entry is at most i, repeats allowed.
All inputs are finite; a program needn't handle non-finite values.
Results may differ from the reference program's by a relative error of at most 0.017.
Values may be sent and summed in bfloat16 or wider, within the bound.
No kernel may reach another device: no remote copies, remote signals or barrier semaphores. Data moves between devices by JAX's collectives and lax.ppermute only.
A program may use at most 128 MiB of HBM per device.

```python
import jax
import jax.numpy as jnp
from jax import lax

HEADS = 16
HEAD_FEATURES = 72
WIDTH = 1152
PATCHES = 512
BLOCK_PATCHES = 64
SPACE_PICKS = 4
BLOCK_FRAMES = 2
TIME_PICKS = 4
FRAMES = 16
CLIPS = 4
SPACE_BLOCKS = 8
TIME_BLOCKS = 8


def draw_space_pattern(key, part):
    others = jax.random.randint(jax.random.fold_in(key, 17), (SPACE_BLOCKS, SPACE_PICKS - 1), 0, SPACE_BLOCKS)
    own_block = jnp.arange(SPACE_BLOCKS, dtype=jnp.int32)[:, None]
    return jnp.concatenate([own_block, others.astype(jnp.int32)], axis=1)


def draw_time_pattern(key, part):
    upper = jnp.arange(1, TIME_BLOCKS + 1, dtype=jnp.int32)[:, None]
    others = jax.random.randint(jax.random.fold_in(key, 29), (TIME_BLOCKS, TIME_PICKS - 1), 0, upper)
    own_block = jnp.arange(TIME_BLOCKS, dtype=jnp.int32)[:, None]
    return jnp.concatenate([own_block, others.astype(jnp.int32)], axis=1)


def shard_levels(own_key, extent, shards, low, top_value):
    level = 1.0
    for dim, shards_of in shards:
        draws = jax.random.uniform(jax.random.fold_in(jax.random.fold_in(own_key, 6), dim), (shards_of,), jnp.float32, low / len(shards), top_value / len(shards))
        level = level * jnp.repeat(jnp.exp(draws), extent[dim] // shards_of).reshape((-1,) + (1,) * (len(extent) - 1 - dim))
    return level


def bell_draw(key, shape, scale, most, split=(), kind=jnp.bfloat16):
    level = shard_levels(key, shape, split, -0.22, 0.18) if split else 1.0
    entries = jax.random.normal(key, shape, jnp.float32) * scale * level
    return jnp.minimum(jnp.maximum(entries, -most), most).astype(kind)


def setup_inputs(seed: int = 0) -> dict:
    seeds = jax.random.split(jax.random.key(seed), 8)
    return {
        "clips": bell_draw(seeds[0], (CLIPS, FRAMES, PATCHES, WIDTH), 1.0, 6.0, ((0, 4), (1, 8))),
        "w_space_qkv": bell_draw(seeds[1], (WIDTH, 3 * WIDTH), WIDTH ** -0.5, 0.1875, ((0, 4),)),
        "w_space_out": bell_draw(seeds[2], (WIDTH, WIDTH), (WIDTH // 32) ** -0.5, 1.0, ((0, 4),)),
        "w_time_qkv": bell_draw(seeds[3], (WIDTH, 3 * WIDTH), WIDTH ** -0.5, 0.1875, ((0, 4),)),
        "w_time_out": bell_draw(seeds[4], (WIDTH, WIDTH), (WIDTH // 32) ** -0.5, 1.0, ((0, 4),)),
        "space_pattern": draw_space_pattern(jax.random.fold_in(seeds[7], 71), 0),
        "time_pattern": draw_time_pattern(jax.random.fold_in(seeds[7], 71), 0),
    }


def layer_norm(values):
    average = lax.optimization_barrier(jnp.mean(values, axis=-1, keepdims=True))
    centred = values - average
    variance = lax.optimization_barrier(jnp.mean(centred * centred, axis=-1, keepdims=True))
    return centred * lax.rsqrt(variance + 1e-06)

def head_norm(values):
    return values * lax.rsqrt(lax.optimization_barrier(jnp.mean(values * values, axis=-1, keepdims=True)) + 1e-06)

def split_heads(packed):
    width = packed.shape[-1] // 3
    leading = packed.shape[:-1]
    query_part = packed[..., :width].reshape(leading + (HEADS, HEAD_FEATURES))
    key_part = packed[..., width:2 * width].reshape(leading + (HEADS, HEAD_FEATURES))
    value_part = packed[..., 2 * width:].reshape(leading + (HEADS, HEAD_FEATURES))
    query_rows = head_norm(query_part.astype(jnp.float32)).astype(jnp.bfloat16)
    incoming_keys = head_norm(key_part.astype(jnp.float32)).astype(jnp.bfloat16)
    return (query_rows, incoming_keys, value_part)

def block_allowed(pattern, count, repeat):
    hits = pattern[:, :, None] == jnp.arange(count, dtype=jnp.int32)[None, None, :]
    blocks = jnp.any(hits, axis=1)
    return jnp.repeat(jnp.repeat(blocks, repeat, axis=0), repeat, axis=1)

def spatial_attend(packed, allowed):
    query_rows, incoming_keys, incoming_values = split_heads(packed)
    logit_scores = jnp.einsum('pxg,exg->xpe', query_rows.astype(jnp.float32), incoming_keys.astype(jnp.float32)) * HEAD_FEATURES ** (-0.5)
    softmax_weights = jnp.where(allowed[None], jnp.exp(logit_scores), 0.0)
    totals = lax.optimization_barrier(jnp.sum(softmax_weights, axis=-1))
    rounded_scores = lax.optimization_barrier(softmax_weights.astype(jnp.bfloat16)).astype(jnp.float32)
    blended_values = jnp.einsum('fok,kfv->ofv', rounded_scores, incoming_values.astype(jnp.float32))
    blended_values = blended_values / jnp.transpose(totals)[:, :, None]
    return blended_values.reshape(packed.shape[0], -1).astype(jnp.bfloat16)

def temporal_attend(packed, allowed):
    query_rows, incoming_keys, incoming_values = split_heads(packed)
    logit_scores = jnp.einsum('fphd,gphd->phfg', query_rows.astype(jnp.float32), incoming_keys.astype(jnp.float32)) * HEAD_FEATURES ** (-0.5)
    softmax_weights = jnp.where(allowed[None, None], jnp.exp(logit_scores), 0.0)
    totals = lax.optimization_barrier(jnp.sum(softmax_weights, axis=-1))
    rounded_scores = lax.optimization_barrier(softmax_weights.astype(jnp.bfloat16)).astype(jnp.float32)
    blended_values = jnp.einsum('phfg,gphd->fphd', rounded_scores, incoming_values.astype(jnp.float32))
    blended_values = blended_values / jnp.transpose(totals, (2, 0, 1))[..., None]
    return blended_values.reshape(packed.shape[0], packed.shape[1], -1).astype(jnp.bfloat16)

def reference(clips, w_space_qkv, w_space_out, w_time_qkv, w_time_out, space_pattern, time_pattern):
    space_allowed = block_allowed(space_pattern, SPACE_BLOCKS, BLOCK_PATCHES)
    time_allowed = block_allowed(time_pattern, TIME_BLOCKS, BLOCK_FRAMES)

    def frame_attend(frame_rows):
        return spatial_attend(frame_rows, space_allowed)

    def one_clip(clip_rows):
        normed = layer_norm(clip_rows.astype(jnp.float32)).astype(jnp.bfloat16).reshape(FRAMES * PATCHES, WIDTH)
        packed = jnp.dot(normed, w_space_qkv, preferred_element_type=jnp.float32).astype(jnp.bfloat16)
        packed = packed.reshape(FRAMES, PATCHES, 3 * WIDTH)
        attended = lax.map(frame_attend, packed)
        branch = jnp.dot(attended.reshape(FRAMES * PATCHES, WIDTH), w_space_out, preferred_element_type=jnp.float32)
        hidden = (clip_rows.astype(jnp.float32) + branch.reshape(FRAMES, PATCHES, WIDTH)).astype(jnp.bfloat16)
        time_normed = layer_norm(hidden.astype(jnp.float32)).astype(jnp.bfloat16).reshape(FRAMES * PATCHES, WIDTH)
        time_packed = jnp.dot(time_normed, w_time_qkv, preferred_element_type=jnp.float32).astype(jnp.bfloat16)
        time_packed = time_packed.reshape(FRAMES, PATCHES, 3 * WIDTH)
        time_attended = temporal_attend(time_packed, time_allowed)
        time_branch = jnp.dot(time_attended.reshape(FRAMES * PATCHES, WIDTH), w_time_out, preferred_element_type=jnp.float32)
        return (hidden.astype(jnp.float32) + time_branch.reshape(FRAMES, PATCHES, WIDTH)).astype(jnp.bfloat16)
    return lax.map(one_clip, clips)
```

```python
from functools import partial

import jax
import jax.numpy as jnp
from jax import lax
from jax.experimental import pallas as pl
from jax.experimental.pallas import tpu as pltpu
from jax.sharding import PartitionSpec as P

HEADS = 16
HEAD_FEATURES = 72
WIDTH = 1152
CHUNKS = 2
LANES = 128
VMEM_LIMIT = 56 * 1024 * 1024
QUERY_SCALE = HEAD_FEATURES**-0.5 * 1.4426950408889634

F32 = jnp.float32
BF16 = jnp.bfloat16


def dot(left, right):
    return jnp.dot(left, right, preferred_element_type=F32)


def dot_rows(left, right):
    return lax.dot_general(left, right, (((1,), (1,)), ((), ())), preferred_element_type=F32)


def layer_norm(values):
    average = jnp.mean(values, axis=-1, keepdims=True)
    centred = values - average
    variance = jnp.mean(centred * centred, axis=-1, keepdims=True)
    return centred * lax.rsqrt(variance + 1e-06)


def iota(shape, dim):
    return lax.broadcasted_iota(jnp.int32, shape, dim)


def head_gather():
    feature, column = iota((WIDTH, LANES), 0), iota((WIDTH, LANES), 1)
    head = jnp.where(column >= HEADS, column - HEADS, column)
    start = head * HEAD_FEATURES
    inside = (feature >= start) & (feature < start + HEAD_FEATURES) & (column < 2 * HEADS)
    return jnp.where(inside, 1.0, 0.0).astype(BF16)


def head_spread():
    column, feature = iota((LANES, WIDTH), 0), iota((LANES, WIDTH), 1)
    head = jnp.where(column >= HEADS, column - HEADS, column)
    start = head * HEAD_FEATURES
    inside = (feature >= start) & (feature < start + HEAD_FEATURES) & (column < 2 * HEADS)
    return jnp.where(inside, 1.0, 0.0).astype(BF16)


def head_norm(packed, gather, spread, scale):
    values = packed.astype(F32)
    squares = dot((values * values).astype(BF16), gather) * (1.0 / HEAD_FEATURES)
    factor = lax.rsqrt(squares + 1e-06) * scale
    high = factor.astype(BF16)
    low = (factor - high.astype(F32)).astype(BF16)
    column = iota(factor.shape, 1)
    both = jnp.where(column < HEADS, high.astype(F32), jnp.where(column < 2 * HEADS, low.astype(F32), 0.0))
    return (values * dot(both.astype(BF16), spread)).astype(BF16)


def block_table(pattern):
    blocks, picks = pattern.shape
    column = iota((blocks, LANES), 1)
    hits = column == pattern[:, 0:1]
    for pick in range(1, picks):
        hits = hits | (column == pattern[:, pick : pick + 1])
    return jnp.where(hits, 1.0, 0.0)


def block_mask(table, query_block, key_block):
    blocks = table.shape[0]
    queries, keys = query_block.shape[0], key_block.shape[0]
    query_hot = jnp.where(query_block == iota((queries, blocks), 1), 1.0, 0.0)
    key_hot = jnp.where(key_block == iota((keys, LANES), 1), 1.0, 0.0)
    return dot_rows(dot(query_hot, table), key_hot)


def shift_of(size):
    assert size & (size - 1) == 0
    return size.bit_length() - 1


def head_window(head):
    first = head * HEAD_FEATURES
    tile = first // LANES
    width = LANES if (first + HEAD_FEATURES - 1) // LANES == tile else 2 * LANES
    return tile * LANES, width, first - tile * LANES


def attend(query_of, key_of, value_of, mask, store):
    for head in range(HEADS):
        start, width, offset = head_window(head)
        window = slice(start, start + width)
        keys, values = key_of(window), value_of(window)
        lane = iota((1, width), 1)
        inside = (lane >= offset) & (lane < offset + HEAD_FEATURES)
        spare = 0 if offset > 0 else HEAD_FEATURES
        marks = jnp.where(inside, 1.0, 0.0).astype(BF16)
        ones = jnp.where(lane == spare, 1.0, 0.0).astype(BF16)
        scores = dot_rows(query_of(window), keys * marks)
        weights = jnp.exp2(scores).astype(BF16) * mask
        blended = dot(weights, values * marks + ones)
        blended = blended * (1.0 / blended[:, spare : spare + 1])
        store(window, inside, blended.astype(BF16))


def merge(ref, row, window, inside, blended):
    old = ref[row, window]
    ref[row, window] = jnp.where(jnp.broadcast_to(inside, blended.shape), blended, old)


def shard_copies(refs, columns, scratch, sem):
    me = lax.axis_index("dp")
    copies = []
    rows = refs[0].shape[0]
    for k, ref in enumerate(refs):
        source = ref if columns is None or ref.shape[1] == scratch.shape[1] else ref.at[:, columns]
        place = pl.multiple_of(jnp.bitwise_xor(me, k) * rows, 16)
        copies.append(pltpu.make_async_copy(source, scratch.at[pl.ds(place, rows), :], sem.at[k]))
    return copies


def start_all(copies):
    for copy in copies:
        copy.start()


def wait_all(copies):
    for copy in copies:
        copy.wait()


def space_qk_kernel(n, x_ref, *refs):
    w_refs, (qk_ref, normed_ref, weight, sem) = refs[:n], refs[n:]
    copies = shard_copies(w_refs, slice(0, 2 * WIDTH), weight, sem)

    @pl.when(pl.program_id(0) == 0)
    def _():
        start_all(copies)

    normed = layer_norm(x_ref[...].astype(F32)).astype(BF16)
    normed_ref[...] = normed
    gather, spread = head_gather(), head_spread()

    @pl.when(pl.program_id(0) == 0)
    def _():
        wait_all(copies)

    for part, scale in ((0, QUERY_SCALE), (1, 1.0)):
        columns = slice(part * WIDTH, (part + 1) * WIDTH)
        packed = dot(normed, weight[:, columns]).astype(BF16)
        qk_ref[:, columns] = head_norm(packed, gather, spread, scale)


def space_v_kernel(n, normed_ref, *refs):
    w_refs, (v_ref, weight, sem) = refs[:n], refs[n:]
    copies = shard_copies(w_refs, slice(2 * WIDTH, 3 * WIDTH), weight, sem)

    @pl.when(pl.program_id(0) == 0)
    def _():
        start_all(copies)
        wait_all(copies)

    v_ref[...] = dot(normed_ref[...], weight[...]).astype(BF16)


def space_attend_kernel(n, first_row, q_ref, k_ref, v_ref, x_ref, pattern_ref, *refs):
    w_refs, (hidden_ref, weight, attended, sem) = refs[:n], refs[n:]
    copies = shard_copies(w_refs, None, weight, sem)

    @pl.when(pl.program_id(0) == 0)
    def _():
        start_all(copies)

    rows, patches = q_ref.shape[1], k_ref.shape[1]
    pattern = pattern_ref[...]
    shift = shift_of(patches // pattern.shape[0])
    query_block = (iota((rows, 1), 0) + first_row) >> shift
    key_block = iota((patches, 1), 0) >> shift
    mask = block_mask(block_table(pattern), query_block, key_block).astype(BF16)
    attend(
        lambda window: q_ref[0, :, window],
        lambda window: k_ref[0, :, window],
        lambda window: v_ref[0, :, window],
        mask,
        lambda window, inside, blended: merge(attended, slice(0, rows), window, inside, blended),
    )

    @pl.when(pl.program_id(0) == 0)
    def _():
        wait_all(copies)

    branch = dot(attended[...], weight[...])
    hidden = (x_ref[0].astype(F32) + branch).astype(BF16)
    hidden_ref[...] = hidden.reshape(hidden_ref.shape)


def time_kernel(n, patches_here, x_ref, pattern_ref, *refs):
    qkv_refs, out_refs, refs = refs[:n], refs[n : 2 * n], refs[2 * n :]
    out_ref, w_qkv, w_out, q_s, k_s, v_s, attended, qkv_sem, out_sem = refs
    qkv_copies = shard_copies(qkv_refs, None, w_qkv, qkv_sem)
    out_copies = shard_copies(out_refs, None, w_out, out_sem)
    start_all(qkv_copies)
    start_all(out_copies)
    rows = x_ref.shape[0]
    frames = rows // patches_here
    tile_patches = 16 if patches_here % 16 == 0 else patches_here
    tile = tile_patches * frames
    pattern = pattern_ref[...]
    shift = shift_of(tile_patches)
    block_shift = shift_of(frames // pattern.shape[0]) + shift
    block = iota((tile, 1), 0) >> block_shift
    allowed = block_mask(block_table(pattern), block, block)
    same = (iota((tile, tile), 0) & (tile_patches - 1)) == (iota((tile, tile), 1) & (tile_patches - 1))
    mask = jnp.where(same, allowed, 0.0).astype(BF16)
    gather, spread = head_gather(), head_spread()
    normed = layer_norm(x_ref[...].astype(F32)).astype(BF16)
    wait_all(qkv_copies)
    q_s[...] = head_norm(dot(normed, w_qkv[:, :WIDTH]).astype(BF16), gather, spread, QUERY_SCALE)
    k_s[...] = head_norm(dot(normed, w_qkv[:, WIDTH : 2 * WIDTH]).astype(BF16), gather, spread, 1.0)
    v_s[...] = dot(normed, w_qkv[:, 2 * WIDTH :]).astype(BF16)

    for first in range(0, patches_here, tile_patches):

        def rows_of(ref, window):
            if tile_patches == patches_here:
                return ref[:, window]
            return jnp.concatenate(
                [ref[pl.ds(f * patches_here + first, tile_patches), window] for f in range(frames)], axis=0
            )

        def store(window, inside, blended):
            if tile_patches == patches_here:
                merge(attended, slice(0, rows), window, inside, blended)
                return
            for f in range(frames):
                merge(
                    attended,
                    pl.ds(f * patches_here + first, tile_patches),
                    window,
                    inside,
                    blended[f * tile_patches : (f + 1) * tile_patches],
                )

        attend(
            partial(rows_of, q_s), partial(rows_of, k_s), partial(rows_of, v_s), mask, store
        )

    wait_all(out_copies)
    branch = dot(attended[...], w_out[...])
    out_ref[...] = (x_ref[...].astype(F32) + branch).astype(BF16)


HBM = pl.BlockSpec(memory_space=pl.ANY)
WHOLE = pl.BlockSpec(memory_space=pltpu.VMEM)


def params(**more):
    return pltpu.CompilerParams(vmem_limit_bytes=VMEM_LIMIT, **more)


def cost(rows, depth, columns, extra=0):
    return pl.CostEstimate(
        flops=2 * rows * depth * columns + extra,
        bytes_accessed=2 * (rows * depth + depth * columns + rows * columns),
        transcendentals=0,
    )


def space_qk(rows_in, shards_of):
    rows, n, step = rows_in.shape[0], len(shards_of), 256
    return pl.pallas_call(
        partial(space_qk_kernel, n),
        grid=(rows // step,),
        in_specs=[pl.BlockSpec((step, WIDTH), lambda i: (i, 0))] + [HBM] * n,
        out_specs=[
            pl.BlockSpec((step, 2 * WIDTH), lambda i: (i, 0)),
            pl.BlockSpec((step, WIDTH), lambda i: (i, 0)),
        ],
        out_shape=[
            jax.ShapeDtypeStruct((rows, 2 * WIDTH), BF16),
            jax.ShapeDtypeStruct((rows, WIDTH), BF16),
        ],
        scratch_shapes=[pltpu.VMEM((WIDTH, 2 * WIDTH), BF16), pltpu.SemaphoreType.DMA((n,))],
        compiler_params=params(),
        cost_estimate=cost(rows, WIDTH, 2 * WIDTH),
        name="space_qk",
    )(rows_in, *shards_of)


def space_v(normed, shards_of):
    rows, n, step = normed.shape[0], len(shards_of), 256
    return pl.pallas_call(
        partial(space_v_kernel, n),
        grid=(rows // step,),
        in_specs=[pl.BlockSpec((step, WIDTH), lambda i: (i, 0))] + [HBM] * n,
        out_specs=pl.BlockSpec((step, WIDTH), lambda i: (i, 0)),
        out_shape=jax.ShapeDtypeStruct((rows, WIDTH), BF16),
        scratch_shapes=[pltpu.VMEM((WIDTH, WIDTH), BF16), pltpu.SemaphoreType.DMA((n,))],
        compiler_params=params(),
        cost_estimate=cost(rows, WIDTH, WIDTH),
        name="space_v",
    )(normed, *shards_of)


def space_attend(chunk, peers, qk, v, clips, pattern, shards_of):
    frames, patches = qk.shape[0], qk.shape[1]
    rows, n = patches // CHUNKS, len(shards_of)
    each = rows // peers
    direct = each % 16 == 0
    if direct:
        out_spec = pl.BlockSpec((peers, 1, each, WIDTH), lambda f: (0, f, 0, 0))
        out_shape = jax.ShapeDtypeStruct((peers, frames, each, WIDTH), BF16)
    else:
        out_spec = pl.BlockSpec((1, rows, WIDTH), lambda f: (f, 0, 0))
        out_shape = jax.ShapeDtypeStruct((frames, rows, WIDTH), BF16)
    hidden = pl.pallas_call(
        partial(space_attend_kernel, n, chunk * rows),
        grid=(frames,),
        in_specs=[
            pl.BlockSpec((1, rows, WIDTH), lambda f: (f, chunk, 0)),
            pl.BlockSpec((1, patches, WIDTH), lambda f: (f, 0, 1)),
            pl.BlockSpec((1, patches, WIDTH), lambda f: (f, 0, 0)),
            pl.BlockSpec((1, rows, WIDTH), lambda f: (f, chunk, 0)),
            WHOLE,
        ]
        + [HBM] * n,
        out_specs=out_spec,
        out_shape=out_shape,
        scratch_shapes=[
            pltpu.VMEM((WIDTH, WIDTH), BF16),
            pltpu.VMEM((rows, WIDTH), BF16),
            pltpu.SemaphoreType.DMA((n,)),
        ],
        compiler_params=params(),
        cost_estimate=cost(frames * rows, WIDTH, WIDTH, frames * rows * patches * HEADS * 4 * 256),
        name=f"space_attend_{chunk}",
    )(qk, qk, v, clips, pattern, *shards_of)
    if direct:
        return hidden
    return jnp.swapaxes(hidden.reshape(frames, peers, each, WIDTH), 0, 1)


def time_branch(chunk, moved, patches_here, pattern, qkv_shards, out_shards):
    rows, n = moved.shape[0], len(qkv_shards)
    return pl.pallas_call(
        partial(time_kernel, n, patches_here),
        in_specs=[WHOLE, WHOLE] + [HBM] * (2 * n),
        out_specs=WHOLE,
        out_shape=jax.ShapeDtypeStruct((rows, WIDTH), BF16),
        scratch_shapes=[
            pltpu.VMEM((WIDTH, 3 * WIDTH), BF16),
            pltpu.VMEM((WIDTH, WIDTH), BF16),
        ]
        + [pltpu.VMEM((rows, WIDTH), BF16)] * 4
        + [pltpu.SemaphoreType.DMA((n,))] * 2,
        compiler_params=params(),
        cost_estimate=cost(rows, WIDTH, 5 * WIDTH),
        name=f"time_branch_{chunk}",
    )(moved, pattern, *qkv_shards, *out_shards)


def swap(value, mask):
    size = lax.axis_size("dp")
    return lax.ppermute(value, "dp", [(i, i ^ mask) for i in range(size)])


def gather_shards(own, remote=None):
    size = lax.axis_size("dp")
    remote = own if remote is None else remote
    shards_of = [own, swap(own, 1)]
    for k in range(2, size, 2):
        there = swap(remote, k)
        shards_of += [there, swap(there, 1)]
    return shards_of


def shards(clips, w_space_qkv, w_space_out, w_time_qkv, w_time_out, space_pattern, time_pattern):
    peers = lax.axis_size("tm")
    frames, patches = clips.shape[1], clips.shape[2]
    frames_all = frames * peers
    each = patches // CHUNKS // peers
    local = clips.reshape(frames, patches, WIDTH)

    own_mate = swap(w_space_qkv, 1)
    qk_there = swap(w_space_qkv[:, : 2 * WIDTH], 2)
    v_there = swap(w_space_qkv[:, 2 * WIDTH :], 2)
    space_out = gather_shards(w_space_out)
    time_qkv = gather_shards(w_time_qkv)
    time_out = gather_shards(w_time_out)

    qk, normed = space_qk(
        local.reshape(frames * patches, WIDTH), [w_space_qkv, own_mate, qk_there, swap(qk_there, 1)]
    )
    v = space_v(normed, [w_space_qkv, own_mate, v_there, swap(v_there, 1)])
    qk = qk.reshape(frames, patches, 2 * WIDTH)
    v = v.reshape(frames, patches, WIDTH)
    returned = []
    for chunk in range(CHUNKS):
        hidden = space_attend(chunk, peers, qk, v, local, space_pattern, space_out)
        moved = lax.all_to_all(hidden, "tm", split_axis=0, concat_axis=0, tiled=True)
        moved = moved.reshape(frames_all * each, WIDTH)
        finished = time_branch(chunk, moved, each, time_pattern, time_qkv, time_out)
        finished = finished.reshape(peers, frames, each, WIDTH)
        back = lax.all_to_all(finished, "tm", split_axis=0, concat_axis=0, tiled=True)
        returned.append(jnp.swapaxes(back, 0, 1).reshape(frames, patches // CHUNKS, WIDTH))
    return jnp.concatenate(returned, axis=1)[None]


def solution(mesh):
    return jax.shard_map(
        shards,
        mesh=mesh,
        in_specs=(
            P("dp", "tm", None, None),
            P("dp", None),
            P("dp", None),
            P("dp", None),
            P("dp", None),
            P(),
            P(),
        ),
        out_specs=P("dp", "tm", None, None),
        check_vma=False,
    )
```

```python
from functools import partial

import jax
import jax.numpy as jnp
from jax import lax
from jax.experimental import pallas as pl
from jax.experimental.pallas import tpu as pltpu
from jax.sharding import PartitionSpec as P

HEADS = 16
HEAD_FEATURES = 72
WIDTH = 1152
CHUNKS = 2
NEAR = 2
LANES = 128
MIB = 1024 * 1024
QUERY_SCALE = HEAD_FEATURES**-0.5 * 1.4426950408889634

F32 = jnp.float32
BF16 = jnp.bfloat16


def dot(left, right):
    return jnp.dot(left, right, preferred_element_type=F32)


def dot_rows(left, right):
    return lax.dot_general(left, right, (((1,), (1,)), ((), ())), preferred_element_type=F32)


def layer_norm(values):
    average = jnp.mean(values, axis=-1, keepdims=True)
    centred = values - average
    variance = jnp.mean(centred * centred, axis=-1, keepdims=True)
    return centred * lax.rsqrt(variance + 1e-06)


def iota(shape, dim):
    return lax.broadcasted_iota(jnp.int32, shape, dim)


def head_gather():
    feature, column = iota((WIDTH, LANES), 0), iota((WIDTH, LANES), 1)
    head = jnp.where(column >= HEADS, column - HEADS, column)
    start = head * HEAD_FEATURES
    inside = (feature >= start) & (feature < start + HEAD_FEATURES) & (column < 2 * HEADS)
    return jnp.where(inside, 1.0, 0.0).astype(BF16)


def head_spread():
    column, feature = iota((LANES, WIDTH), 0), iota((LANES, WIDTH), 1)
    head = jnp.where(column >= HEADS, column - HEADS, column)
    start = head * HEAD_FEATURES
    inside = (feature >= start) & (feature < start + HEAD_FEATURES) & (column < 2 * HEADS)
    return jnp.where(inside, 1.0, 0.0).astype(BF16)


def head_norm(packed, gather, spread, scale):
    values = packed.astype(F32)
    squares = dot((values * values).astype(BF16), gather) * (1.0 / HEAD_FEATURES)
    factor = lax.rsqrt(squares + 1e-06) * scale
    high = factor.astype(BF16)
    low = (factor - high.astype(F32)).astype(BF16)
    column = iota(factor.shape, 1)
    both = jnp.where(column < HEADS, high.astype(F32), jnp.where(column < 2 * HEADS, low.astype(F32), 0.0))
    return (values * dot(both.astype(BF16), spread)).astype(BF16)


def block_table(picks):
    blocks = picks.shape[1]
    row = iota((blocks, blocks), 0)
    hits = row == picks[0:1]
    for pick in range(1, picks.shape[0]):
        hits = hits | (row == picks[pick : pick + 1])
    return jnp.where(hits, 1.0, 0.0)


def block_mask(table, query_block, key_block):
    blocks = table.shape[0]
    queries, keys = query_block.shape[0], key_block.shape[0]
    query_hot = jnp.where(query_block == iota((queries, blocks), 1), 1.0, 0.0)
    key_hot = jnp.where(key_block == iota((keys, blocks), 1), 1.0, 0.0)
    return dot_rows(dot_rows(query_hot, table), key_hot)


def shift_of(size):
    assert size & (size - 1) == 0
    return size.bit_length() - 1


def head_window(head):
    first = head * HEAD_FEATURES
    tile = first // LANES
    width = LANES if (first + HEAD_FEATURES - 1) // LANES == tile else 2 * LANES
    return tile * LANES, width, first - tile * LANES


def attend(query_of, key_of, value_of, mask, store):
    for head in range(HEADS):
        start, width, offset = head_window(head)
        window = slice(start, start + width)
        keys, values = key_of(window), value_of(window)
        lane = iota((1, width), 1)
        inside = (lane >= offset) & (lane < offset + HEAD_FEATURES)
        spare = 0 if offset > 0 else HEAD_FEATURES
        marks = jnp.where(inside, 1.0, 0.0).astype(BF16)
        ones = jnp.where(lane == spare, 1.0, 0.0).astype(BF16)
        scores = dot_rows(query_of(window), keys * marks)
        weights = jnp.exp2(scores).astype(BF16) * mask
        blended = dot(weights, values * marks + ones)
        blended = blended * (1.0 / blended[:, spare : spare + 1])
        store(window, inside, blended.astype(BF16))


def merge(ref, row, window, inside, blended):
    old = ref[row, window]
    ref[row, window] = jnp.where(jnp.broadcast_to(inside, blended.shape), blended, old)


def lay_shards(refs, near, column, weight, sem):
    me = lax.axis_index("dp")
    rows, width = refs[0].shape[0], weight.shape[1]
    copies = []
    for k, ref in enumerate(refs):
        place = weight.at[pl.ds(pl.multiple_of(jnp.bitwise_xor(me, k) * rows, 16), rows), :]
        if k < near:
            source = ref if ref.shape[1] == width else ref.at[:, pl.ds(column, width)]
            copies.append(pltpu.make_async_copy(source, place, sem.at[k]))
            copies[-1].start()
        else:
            place[...] = ref[...]
    return copies


def wait_all(copies):
    for copy in copies:
        copy.wait()


def norm_kernel(x_ref, out_ref, token_ref):
    out_ref[...] = layer_norm(x_ref[...].astype(F32)).astype(BF16)
    token_ref[...] = jnp.zeros_like(token_ref)


def part_scale(part):
    return jnp.where(part == 0, QUERY_SCALE, 1.0).astype(F32)


def space_first_kernel(n, normed_ref, *refs):
    w_refs, (_, out_ref, token_ref, weight, sem) = refs[:n], refs[n:]
    part = lax.axis_index("tm") & 1

    @pl.when(pl.program_id(0) == 0)
    def _():
        wait_all(lay_shards(w_refs, NEAR, pl.multiple_of(part * WIDTH, LANES), weight, sem))
        token_ref[...] = jnp.zeros_like(token_ref)

    packed = dot(normed_ref[...], weight[...]).astype(BF16)
    out_ref[...] = head_norm(packed, head_gather(), head_spread(), part_scale(part))


def pick_queries(part, first_ref, second_ref, queries, q_s, k_s):
    @pl.when(part == 0)
    def _():
        q_s[...] = first_ref[queries, :]
        k_s[...] = second_ref[...]

    @pl.when(part == 1)
    def _():
        q_s[...] = second_ref[queries, :]
        k_s[...] = first_ref[...]


def space_blocks(first_row, picks, v_ref, out_ref, q_s, k_s):
    rows, patches = q_s.shape[0], k_s.shape[0]
    shift = shift_of(patches // picks.shape[1])
    query_block = (iota((rows, 1), 0) + first_row) >> shift
    key_block = iota((patches, 1), 0) >> shift
    mask = block_mask(block_table(picks), query_block, key_block).astype(BF16)
    attend(
        lambda window: q_s[:, window],
        lambda window: k_s[:, window],
        lambda window: v_ref[:, window],
        mask,
        lambda window, inside, blended: merge(out_ref, slice(0, rows), window, inside, blended),
    )


def space_rest_kernel(n, normed_ref, first_ref, picks_ref, *refs):
    second_refs, v_refs, refs = refs[:n], refs[n : 2 * n], refs[2 * n :]
    _, second_ref, v_ref, out_ref, token_ref, weight, v_weight, q_s, k_s, sem, v_sem = refs
    part = lax.axis_index("tm") & 1

    @pl.when(pl.program_id(0) == 0)
    def _():
        copies = lay_shards(v_refs, NEAR, 2 * WIDTH, v_weight, v_sem)
        copies += lay_shards(second_refs, NEAR, pl.multiple_of((1 - part) * WIDTH, LANES), weight, sem)
        wait_all(copies)
        token_ref[...] = jnp.zeros_like(token_ref)

    normed = normed_ref[...]
    v_ref[...] = dot(normed, v_weight[...]).astype(BF16)
    packed = dot(normed, weight[...]).astype(BF16)
    second_ref[...] = head_norm(packed, head_gather(), head_spread(), part_scale(1 - part))
    pick_queries(part, first_ref, second_ref, pl.ds(0, q_s.shape[0]), q_s, k_s)
    space_blocks(0, picks_ref[...], v_ref, out_ref, q_s, k_s)


def space_attend_kernel(first_row, first_ref, second_ref, v_ref, picks_ref, _, out_ref, q_s, k_s):
    part = lax.axis_index("tm") & 1
    pick_queries(part, first_ref, second_ref, pl.ds(first_row, q_s.shape[0]), q_s, k_s)
    space_blocks(first_row, picks_ref[...], v_ref, out_ref, q_s, k_s)


def space_out_kernel(n, attended_ref, x_ref, *refs):
    w_refs, (hidden_ref, token_ref, weight, sem) = refs[:n], refs[n:]

    @pl.when(pl.program_id(0) == 0)
    def _():
        wait_all(lay_shards(w_refs, NEAR, 0, weight, sem))
        token_ref[...] = jnp.zeros_like(token_ref)

    branch = dot(attended_ref[...], weight[...])
    hidden = (x_ref[...].astype(F32) + branch).astype(BF16)
    hidden_ref[...] = hidden.reshape(hidden_ref.shape)


def time_kernel(patches_here, x_ref, picks_ref, w_ref, _, out_ref, token_ref, weight, q_s, k_s, v_s, attended, sem):
    token_ref[...] = jnp.zeros_like(token_ref)
    copies = []
    for part in range(4):
        columns = pl.ds(part * WIDTH, WIDTH)
        copies.append(pltpu.make_async_copy(w_ref.at[:, columns], weight.at[:, columns], sem.at[part]))
        copies[-1].start()
    rows = x_ref.shape[0]
    frames = rows // patches_here
    tile_patches = 16 if patches_here % 16 == 0 else patches_here
    tile = tile_patches * frames
    pattern = picks_ref[...]
    shift = shift_of(tile_patches)
    block_shift = shift_of(frames // pattern.shape[1]) + shift
    block = iota((tile, 1), 0) >> block_shift
    allowed = block_mask(block_table(pattern), block, block)
    same = (iota((tile, tile), 0) & (tile_patches - 1)) == (iota((tile, tile), 1) & (tile_patches - 1))
    mask = jnp.where(same, allowed, 0.0).astype(BF16)
    gather, spread = head_gather(), head_spread()
    normed = layer_norm(x_ref[...].astype(F32)).astype(BF16)
    copies[0].wait()
    q_s[...] = head_norm(dot(normed, weight[:, :WIDTH]).astype(BF16), gather, spread, QUERY_SCALE)
    copies[1].wait()
    k_s[...] = head_norm(dot(normed, weight[:, WIDTH : 2 * WIDTH]).astype(BF16), gather, spread, 1.0)
    copies[2].wait()
    v_s[...] = dot(normed, weight[:, 2 * WIDTH : 3 * WIDTH]).astype(BF16)

    for first in range(0, patches_here, tile_patches):

        def rows_of(ref, window):
            if tile_patches == patches_here:
                return ref[:, window]
            return jnp.concatenate(
                [ref[pl.ds(f * patches_here + first, tile_patches), window] for f in range(frames)], axis=0
            )

        def store(window, inside, blended):
            if tile_patches == patches_here:
                merge(attended, slice(0, rows), window, inside, blended)
                return
            for f in range(frames):
                merge(
                    attended,
                    pl.ds(f * patches_here + first, tile_patches),
                    window,
                    inside,
                    blended[f * tile_patches : (f + 1) * tile_patches],
                )

        attend(
            partial(rows_of, q_s), partial(rows_of, k_s), partial(rows_of, v_s), mask, store
        )

    copies[3].wait()
    branch = dot(attended[...], weight[:, 3 * WIDTH :])
    out_ref[...] = (x_ref[...].astype(F32) + branch).astype(BF16)


HBM = pl.BlockSpec(memory_space=pl.ANY)
WHOLE = pl.BlockSpec(memory_space=pltpu.VMEM)
TOKEN = jax.ShapeDtypeStruct((8, LANES), F32)
TOKEN_SPEC = pl.BlockSpec((8, LANES), lambda *_: (0, 0))


def params(mib):
    return pltpu.CompilerParams(vmem_limit_bytes=mib * MIB)


def cost(rows, depth, columns, extra=0):
    return pl.CostEstimate(flops=rows * depth * columns // 8, bytes_accessed=2 * rows * columns // 8, transcendentals=0)


def norm_rows(rows_in):
    rows, step = rows_in.shape[0], 256
    spec = pl.BlockSpec((step, WIDTH), lambda i: (i, 0))
    return pl.pallas_call(
        norm_kernel,
        grid=(rows // step,),
        in_specs=[spec],
        out_specs=[spec, TOKEN_SPEC],
        out_shape=[jax.ShapeDtypeStruct((rows, WIDTH), BF16), TOKEN],
        compiler_params=params(10),
        name="norm_rows",
    )(rows_in)


def shard_specs(n):
    return [HBM] * NEAR + [WHOLE] * (n - NEAR)


def space_first(normed, shards_of, token):
    rows, n, step = normed.shape[0], len(shards_of), 256
    flat = pl.BlockSpec((step, WIDTH), lambda i: (i, 0))
    return pl.pallas_call(
        partial(space_first_kernel, n),
        grid=(rows // step,),
        in_specs=[flat] + shard_specs(n) + [HBM],
        out_specs=[flat, TOKEN_SPEC],
        out_shape=[jax.ShapeDtypeStruct((rows, WIDTH), BF16), TOKEN],
        scratch_shapes=[pltpu.VMEM((WIDTH, WIDTH), BF16), pltpu.SemaphoreType.DMA((NEAR,))],
        compiler_params=params(14),
        cost_estimate=cost(rows, WIDTH, WIDTH),
        name="space_first",
    )(normed, *shards_of, token)


def space_rest(frames, normed, first, second_shards, v_shards, picks, token):
    n, patches = len(v_shards), normed.shape[0] // frames
    rows = patches // CHUNKS
    frame = pl.BlockSpec((patches, WIDTH), lambda f: (f, 0))
    return pl.pallas_call(
        partial(space_rest_kernel, n),
        grid=(frames,),
        in_specs=[frame, frame, WHOLE] + shard_specs(n) * 2 + [HBM],
        out_specs=[frame, frame, pl.BlockSpec((None, rows, WIDTH), lambda f: (f, 0, 0)), TOKEN_SPEC],
        out_shape=[jax.ShapeDtypeStruct(normed.shape, BF16)] * 2
        + [jax.ShapeDtypeStruct((frames, rows, WIDTH), BF16), TOKEN],
        scratch_shapes=[pltpu.VMEM((WIDTH, WIDTH), BF16)] * 2
        + [pltpu.VMEM((rows, WIDTH), BF16), pltpu.VMEM((patches, WIDTH), BF16)]
        + [pltpu.SemaphoreType.DMA((NEAR,))] * 2,
        compiler_params=params(28),
        cost_estimate=cost(frames * patches, WIDTH, 2 * WIDTH),
        name="space_rest",
    )(normed, first, picks, *second_shards, *v_shards, token)


def space_attend(chunk, frames, first, second, v, picks, token):
    patches = v.shape[0] // frames
    rows = patches // CHUNKS
    frame = pl.BlockSpec((patches, WIDTH), lambda f: (f, 0))
    return pl.pallas_call(
        partial(space_attend_kernel, chunk * rows),
        grid=(frames,),
        in_specs=[frame, frame, frame, WHOLE, HBM],
        out_specs=pl.BlockSpec((None, rows, WIDTH), lambda f: (f, 0, 0)),
        out_shape=jax.ShapeDtypeStruct((frames, rows, WIDTH), BF16),
        scratch_shapes=[pltpu.VMEM((rows, WIDTH), BF16), pltpu.VMEM((patches, WIDTH), BF16)],
        compiler_params=params(18),
        cost_estimate=cost(frames * rows, WIDTH, WIDTH),
        name=f"space_attend_{chunk}",
    )(first, second, v, picks, token)


def space_out(chunk, peers, attended, clips, shards_of):
    frames, rows, n = attended.shape[0], attended.shape[1], len(shards_of)
    each = rows // peers
    direct = each % 16 == 0
    if direct:
        out_spec = pl.BlockSpec((peers, 1, each, WIDTH), lambda f: (0, f, 0, 0))
        shape = (peers, frames, each, WIDTH)
    else:
        out_spec = pl.BlockSpec((None, rows, WIDTH), lambda f: (f, 0, 0))
        shape = (frames, rows, WIDTH)
    hidden, token = pl.pallas_call(
        partial(space_out_kernel, n),
        grid=(frames,),
        in_specs=[
            pl.BlockSpec((None, rows, WIDTH), lambda f: (f, 0, 0)),
            pl.BlockSpec((None, rows, WIDTH), lambda f: (f, chunk, 0)),
        ]
        + shard_specs(n),
        out_specs=[out_spec, TOKEN_SPEC],
        out_shape=[jax.ShapeDtypeStruct(shape, BF16), TOKEN],
        scratch_shapes=[pltpu.VMEM((WIDTH, WIDTH), BF16), pltpu.SemaphoreType.DMA((NEAR,))],
        compiler_params=params(12),
        cost_estimate=cost(frames * rows, WIDTH, WIDTH),
        name=f"space_out_{chunk}",
    )(attended, clips, *shards_of)
    if not direct:
        hidden = jnp.swapaxes(hidden.reshape(frames, peers, each, WIDTH), 0, 1)
    return hidden, token


def time_branch(chunk, moved, patches_here, picks, weight, token):
    rows = moved.shape[0]
    return pl.pallas_call(
        partial(time_kernel, patches_here),
        in_specs=[WHOLE, WHOLE, HBM, HBM],
        out_specs=[WHOLE, WHOLE],
        out_shape=[jax.ShapeDtypeStruct((rows, WIDTH), BF16), TOKEN],
        scratch_shapes=[pltpu.VMEM(weight.shape, BF16)]
        + [pltpu.VMEM((rows, WIDTH), BF16)] * 4
        + [pltpu.SemaphoreType.DMA((4,))],
        compiler_params=params(52),
        cost_estimate=cost(rows, WIDTH, 5 * WIDTH),
        name=f"time_branch_{chunk}",
    )(moved, picks, weight, token)


def swap(value, mask, axis="dp"):
    return lax.ppermute(value, axis, [(i, i ^ mask) for i in range(lax.axis_size(axis))])


def side_by_side_kernel(left_ref, right_ref, _, out_ref):
    last = pl.num_programs(0) - 1

    @pl.when(pl.program_id(0) < last)
    def _():
        out_ref[...] = left_ref[...]

    @pl.when(pl.program_id(0) == last)
    def _():
        out_ref[...] = right_ref[...]


def side_by_side(left, right, token):
    rows, columns = left.shape
    parts = columns // WIDTH
    return pl.pallas_call(
        side_by_side_kernel,
        grid=(parts + 1,),
        in_specs=[
            pl.BlockSpec((rows, WIDTH), lambda i: (0, jnp.minimum(i, parts - 1))),
            pl.BlockSpec((rows, WIDTH), lambda i: (0, 0)),
            HBM,
        ],
        out_specs=pl.BlockSpec((rows, WIDTH), lambda i: (0, i)),
        out_shape=jax.ShapeDtypeStruct((rows, columns + WIDTH), left.dtype),
        compiler_params=params(8),
        name="side_by_side",
    )(left, right, token)


def after(value, other):
    return pl.pallas_call(
        lambda *refs: None,
        in_specs=[HBM] * 2,
        out_specs=HBM,
        out_shape=jax.ShapeDtypeStruct(value.shape, value.dtype),
        input_output_aliases={0: 0},
        compiler_params=params(1),
        name="after",
    )(value, other)


def together(*values):
    n = len(values)
    return pl.pallas_call(
        lambda *refs: None,
        in_specs=[HBM] * n,
        out_specs=[HBM] * n,
        out_shape=[jax.ShapeDtypeStruct(value.shape, value.dtype) for value in values],
        input_output_aliases={i: i for i in range(n)},
        compiler_params=params(1),
        name="together",
    )(*values)


def shards(clips, w_space_qkv, w_space_out, w_time_qkv, w_time_out, space_pattern, time_pattern):
    peers = lax.axis_size("tm")
    frames, patches = clips.shape[1], clips.shape[2]
    frames_all = frames * peers
    each = patches // CHUNKS // peers
    local = clips.reshape(frames, patches, WIDTH)
    space_picks, time_picks = space_pattern.T, time_pattern.T

    part = lax.axis_index("tm") & 1
    first_there = swap(lax.dynamic_slice_in_dim(w_space_qkv, part * WIDTH, WIDTH, 1), 2)
    own_mate = swap(w_space_qkv, 1)
    own = [w_space_qkv, own_mate]
    normed, token = norm_rows(local.reshape(frames * patches, WIDTH))
    first_there, token = together(first_there, token)
    first_mate = swap(first_there, 1)
    second_there = swap(first_there, 1, "tm")
    v_there = swap(w_space_qkv[:, 2 * WIDTH :], 2)
    out_there = swap(w_space_out, 2)
    (token,) = together(token)
    first, token = space_first(normed, own + [first_there, first_mate], token)
    second_there, v_there, token = together(second_there, v_there, token)
    w_time = lax.all_gather(side_by_side(w_time_qkv, w_time_out, token), "dp", axis=0, tiled=True)
    second_mate, v_mate = swap(second_there, 1), swap(v_there, 1)
    (token,) = together(token)
    second, v, attended, token = space_rest(
        frames, normed, first, own + [second_there, second_mate], own + [v_there, v_mate], space_picks, token
    )
    out_there, token = together(out_there, token)
    space_out_shards = [w_space_out, swap(w_space_out, 1), out_there, swap(out_there, 1)]
    moved = []
    for chunk in range(CHUNKS):
        if chunk > 0:
            attended = space_attend(chunk, frames, first, second, v, space_picks, token)
        hidden, token = space_out(chunk, peers, attended, local, space_out_shards)
        moved.append(lax.all_to_all(hidden, "tm", split_axis=0, concat_axis=0, tiled=True))
    returned = []
    for chunk in range(CHUNKS):
        rows = moved[chunk].reshape(frames_all * each, WIDTH)
        finished, token = time_branch(chunk, rows, each, time_picks, w_time, token)
        finished = finished.reshape(peers, frames, each, WIDTH)
        if chunk > 0:
            finished = after(finished, back)
        back = lax.all_to_all(finished, "tm", split_axis=0, concat_axis=0, tiled=True)
        returned.append(jnp.swapaxes(back, 0, 1).reshape(frames, patches // CHUNKS, WIDTH))
    return jnp.concatenate(returned, axis=1)[None]


def solution(mesh):
    return jax.shard_map(
        shards,
        mesh=mesh,
        in_specs=(
            P("dp", "tm", None, None),
            P("dp", None),
            P("dp", None),
            P("dp", None),
            P("dp", None),
            P(),
            P(),
        ),
        out_specs=P("dp", "tm", None, None),
        check_vma=False,
    )
```

```python
from functools import partial

import jax
import jax.numpy as jnp
from jax import lax
from jax.experimental import pallas as pl
from jax.experimental.pallas import tpu as pltpu
from jax.sharding import PartitionSpec as P

HEADS = 16
HEAD_FEATURES = 72
WIDTH = 1152
CHUNKS = 2
NEAR = 2
LANES = 128
MIB = 1024 * 1024
QUERY_SCALE = HEAD_FEATURES**-0.5 * 1.4426950408889634

F32 = jnp.float32
BF16 = jnp.bfloat16


def dot(left, right):
    return jnp.dot(left, right, preferred_element_type=F32)


def dot_rows(left, right):
    return lax.dot_general(left, right, (((1,), (1,)), ((), ())), preferred_element_type=F32)


def layer_norm(values):
    average = jnp.mean(values, axis=-1, keepdims=True)
    centred = values - average
    variance = jnp.mean(centred * centred, axis=-1, keepdims=True)
    return centred * lax.rsqrt(variance + 1e-06)


def iota(shape, dim):
    return lax.broadcasted_iota(jnp.int32, shape, dim)


def head_gather():
    feature, column = iota((WIDTH, LANES), 0), iota((WIDTH, LANES), 1)
    head = jnp.where(column >= HEADS, column - HEADS, column)
    start = head * HEAD_FEATURES
    inside = (feature >= start) & (feature < start + HEAD_FEATURES) & (column < 2 * HEADS)
    return jnp.where(inside, 1.0, 0.0).astype(BF16)


def head_spread():
    column, feature = iota((LANES, WIDTH), 0), iota((LANES, WIDTH), 1)
    head = jnp.where(column >= HEADS, column - HEADS, column)
    start = head * HEAD_FEATURES
    inside = (feature >= start) & (feature < start + HEAD_FEATURES) & (column < 2 * HEADS)
    return jnp.where(inside, 1.0, 0.0).astype(BF16)


def head_norm(packed, gather, spread, scale):
    values = packed.astype(F32)
    squares = dot((values * values).astype(BF16), gather) * (1.0 / HEAD_FEATURES)
    factor = lax.rsqrt(squares + 1e-06) * scale
    high = factor.astype(BF16)
    low = (factor - high.astype(F32)).astype(BF16)
    column = iota(factor.shape, 1)
    both = jnp.where(column < HEADS, high.astype(F32), jnp.where(column < 2 * HEADS, low.astype(F32), 0.0))
    return (values * dot(both.astype(BF16), spread)).astype(BF16)


def block_table(picks):
    blocks = picks.shape[1]
    row = iota((blocks, blocks), 0)
    hits = row == picks[0:1]
    for pick in range(1, picks.shape[0]):
        hits = hits | (row == picks[pick : pick + 1])
    return jnp.where(hits, 1.0, 0.0)


def block_mask(table, query_block, key_block):
    blocks = table.shape[0]
    queries, keys = query_block.shape[0], key_block.shape[0]
    query_hot = jnp.where(query_block == iota((queries, blocks), 1), 1.0, 0.0)
    key_hot = jnp.where(key_block == iota((keys, blocks), 1), 1.0, 0.0)
    return dot_rows(dot_rows(query_hot, table), key_hot)


def shift_of(size):
    assert size & (size - 1) == 0
    return size.bit_length() - 1


def head_window(head):
    first = head * HEAD_FEATURES
    tile = first // LANES
    width = LANES if (first + HEAD_FEATURES - 1) // LANES == tile else 2 * LANES
    return tile * LANES, width, first - tile * LANES


def attend(query_of, key_of, value_of, mask, store):
    for head in range(HEADS):
        start, width, offset = head_window(head)
        window = slice(start, start + width)
        keys, values = key_of(window), value_of(window)
        lane = iota((1, width), 1)
        inside = (lane >= offset) & (lane < offset + HEAD_FEATURES)
        spare = 0 if offset > 0 else HEAD_FEATURES
        marks = jnp.where(inside, 1.0, 0.0).astype(BF16)
        ones = jnp.where(lane == spare, 1.0, 0.0).astype(BF16)
        scores = dot_rows(query_of(window), keys * marks)
        weights = jnp.exp2(scores).astype(BF16) * mask
        blended = dot(weights, values * marks + ones)
        blended = blended * (1.0 / blended[:, spare : spare + 1])
        store(window, inside, blended.astype(BF16))


def merge(ref, row, window, inside, blended):
    old = ref[row, window]
    ref[row, window] = jnp.where(jnp.broadcast_to(inside, blended.shape), blended, old)


def lay_shards(refs, near, column, weight, sem):
    me = lax.axis_index("dp")
    rows, width = refs[0].shape[0], weight.shape[1]
    copies = []
    for k, ref in enumerate(refs):
        place = weight.at[pl.ds(pl.multiple_of(jnp.bitwise_xor(me, k) * rows, 16), rows), :]
        if k < near:
            source = ref if ref.shape[1] == width else ref.at[:, pl.ds(column, width)]
            copies.append(pltpu.make_async_copy(source, place, sem.at[k]))
            copies[-1].start()
        else:
            place[...] = ref[...]
    return copies


def wait_all(copies):
    for copy in copies:
        copy.wait()


def norm_kernel(x_ref, out_ref, token_ref):
    out_ref[...] = layer_norm(x_ref[...].astype(F32)).astype(BF16)
    token_ref[...] = jnp.zeros_like(token_ref)


def part_scale(part):
    return jnp.where(part == 0, QUERY_SCALE, 1.0).astype(F32)


def space_first_kernel(n, normed_ref, *refs):
    w_refs, (_, out_ref, token_ref, weight, sem) = refs[:n], refs[n:]
    part = lax.axis_index("tm") & 1

    @pl.when(pl.program_id(0) == 0)
    def _():
        wait_all(lay_shards(w_refs, NEAR, pl.multiple_of(part * WIDTH, LANES), weight, sem))
        token_ref[...] = jnp.zeros_like(token_ref)

    packed = dot(normed_ref[...], weight[...]).astype(BF16)
    out_ref[...] = head_norm(packed, head_gather(), head_spread(), part_scale(part))


def pick_queries(part, first_ref, second_ref, queries, q_s, k_s):
    @pl.when(part == 0)
    def _():
        q_s[...] = first_ref[queries, :]
        k_s[...] = second_ref[...]

    @pl.when(part == 1)
    def _():
        q_s[...] = second_ref[queries, :]
        k_s[...] = first_ref[...]


def space_blocks(first_row, picks, v_ref, out_ref, q_s, k_s):
    rows, patches = q_s.shape[0], k_s.shape[0]
    shift = shift_of(patches // picks.shape[1])
    query_block = (iota((rows, 1), 0) + first_row) >> shift
    key_block = iota((patches, 1), 0) >> shift
    mask = block_mask(block_table(picks), query_block, key_block).astype(BF16)
    attend(
        lambda window: q_s[:, window],
        lambda window: k_s[:, window],
        lambda window: v_ref[:, window],
        mask,
        lambda window, inside, blended: merge(out_ref, slice(0, rows), window, inside, blended),
    )


def space_rest_kernel(n, normed_ref, first_ref, picks_ref, *refs):
    second_refs, v_refs, refs = refs[:n], refs[n : 2 * n], refs[2 * n :]
    _, second_ref, v_ref, out_ref, token_ref, weight, v_weight, q_s, k_s, sem, v_sem = refs
    part = lax.axis_index("tm") & 1

    @pl.when(pl.program_id(0) == 0)
    def _():
        copies = lay_shards(v_refs, NEAR, 2 * WIDTH, v_weight, v_sem)
        copies += lay_shards(second_refs, NEAR, pl.multiple_of((1 - part) * WIDTH, LANES), weight, sem)
        wait_all(copies)
        token_ref[...] = jnp.zeros_like(token_ref)

    normed = normed_ref[...]
    v_ref[...] = dot(normed, v_weight[...]).astype(BF16)
    packed = dot(normed, weight[...]).astype(BF16)
    second_ref[...] = head_norm(packed, head_gather(), head_spread(), part_scale(1 - part))
    pick_queries(part, first_ref, second_ref, pl.ds(0, q_s.shape[0]), q_s, k_s)
    space_blocks(0, picks_ref[...], v_ref, out_ref, q_s, k_s)


def space_attend_kernel(first_row, first_ref, second_ref, v_ref, picks_ref, _, out_ref, q_s, k_s):
    part = lax.axis_index("tm") & 1
    pick_queries(part, first_ref, second_ref, pl.ds(first_row, q_s.shape[0]), q_s, k_s)
    space_blocks(first_row, picks_ref[...], v_ref, out_ref, q_s, k_s)


def space_out_kernel(n, attended_ref, x_ref, *refs):
    w_refs, (hidden_ref, token_ref, weight, sem) = refs[:n], refs[n:]

    @pl.when(pl.program_id(0) == 0)
    def _():
        wait_all(lay_shards(w_refs, NEAR, 0, weight, sem))
        token_ref[...] = jnp.zeros_like(token_ref)

    branch = dot(attended_ref[...], weight[...])
    hidden = (x_ref[...].astype(F32) + branch).astype(BF16)
    hidden_ref[...] = hidden.reshape(hidden_ref.shape)


def time_kernel(n, patches_here, x_ref, picks_ref, *refs):
    w_refs, (_, attended, token_ref, weight, q_s, k_s, v_s, sem) = refs[:n], refs[n:]
    token_ref[...] = jnp.zeros_like(token_ref)
    copies = [
        lay_shards(w_refs, n, part * WIDTH, weight.at[part], sem.at[part]) for part in range(3)
    ]
    rows = x_ref.shape[0]
    frames = rows // patches_here
    tile_patches = 16 if patches_here % 16 == 0 else patches_here
    tile = tile_patches * frames
    pattern = picks_ref[...]
    shift = shift_of(tile_patches)
    block_shift = shift_of(frames // pattern.shape[1]) + shift
    block = iota((tile, 1), 0) >> block_shift
    allowed = block_mask(block_table(pattern), block, block)
    same = (iota((tile, tile), 0) & (tile_patches - 1)) == (iota((tile, tile), 1) & (tile_patches - 1))
    mask = jnp.where(same, allowed, 0.0).astype(BF16)
    gather, spread = head_gather(), head_spread()
    normed = layer_norm(x_ref[...].astype(F32)).astype(BF16)
    wait_all(copies[0])
    q_s[...] = head_norm(dot(normed, weight[0]).astype(BF16), gather, spread, QUERY_SCALE)
    wait_all(copies[1])
    k_s[...] = head_norm(dot(normed, weight[1]).astype(BF16), gather, spread, 1.0)
    wait_all(copies[2])
    v_s[...] = dot(normed, weight[2]).astype(BF16)

    for first in range(0, patches_here, tile_patches):

        def rows_of(ref, window):
            if tile_patches == patches_here:
                return ref[:, window]
            return jnp.concatenate(
                [ref[pl.ds(f * patches_here + first, tile_patches), window] for f in range(frames)], axis=0
            )

        def store(window, inside, blended):
            if tile_patches == patches_here:
                merge(attended, slice(0, rows), window, inside, blended)
                return
            for f in range(frames):
                merge(
                    attended,
                    pl.ds(f * patches_here + first, tile_patches),
                    window,
                    inside,
                    blended[f * tile_patches : (f + 1) * tile_patches],
                )

        attend(
            partial(rows_of, q_s), partial(rows_of, k_s), partial(rows_of, v_s), mask, store
        )


def time_out_kernel(n, attended_ref, x_ref, *refs):
    w_refs, (_, out_ref, token_ref, weight, sem) = refs[:n], refs[n:]
    wait_all(lay_shards(w_refs, NEAR, 0, weight, sem))
    token_ref[...] = jnp.zeros_like(token_ref)
    out_ref[...] = (x_ref[...].astype(F32) + dot(attended_ref[...], weight[...])).astype(BF16)


HBM = pl.BlockSpec(memory_space=pl.ANY)
WHOLE = pl.BlockSpec(memory_space=pltpu.VMEM)
TOKEN = jax.ShapeDtypeStruct((8, LANES), F32)
TOKEN_SPEC = pl.BlockSpec((8, LANES), lambda *_: (0, 0))


def params(mib):
    return pltpu.CompilerParams(vmem_limit_bytes=mib * MIB)


def cost(rows, depth, columns, extra=0):
    return pl.CostEstimate(flops=rows * depth * columns // 8, bytes_accessed=2 * rows * columns // 8, transcendentals=0)


def norm_rows(rows_in):
    rows, step = rows_in.shape[0], 256
    spec = pl.BlockSpec((step, WIDTH), lambda i: (i, 0))
    return pl.pallas_call(
        norm_kernel,
        grid=(rows // step,),
        in_specs=[spec],
        out_specs=[spec, TOKEN_SPEC],
        out_shape=[jax.ShapeDtypeStruct((rows, WIDTH), BF16), TOKEN],
        compiler_params=params(10),
        name="norm_rows",
    )(rows_in)


def shard_specs(n):
    return [HBM] * NEAR + [WHOLE] * (n - NEAR)


def space_first(normed, shards_of, token):
    rows, n, step = normed.shape[0], len(shards_of), 256
    flat = pl.BlockSpec((step, WIDTH), lambda i: (i, 0))
    return pl.pallas_call(
        partial(space_first_kernel, n),
        grid=(rows // step,),
        in_specs=[flat] + shard_specs(n) + [HBM],
        out_specs=[flat, TOKEN_SPEC],
        out_shape=[jax.ShapeDtypeStruct((rows, WIDTH), BF16), TOKEN],
        scratch_shapes=[pltpu.VMEM((WIDTH, WIDTH), BF16), pltpu.SemaphoreType.DMA((NEAR,))],
        compiler_params=params(14),
        cost_estimate=cost(rows, WIDTH, WIDTH),
        name="space_first",
    )(normed, *shards_of, token)


def space_rest(frames, normed, first, second_shards, v_shards, picks, token):
    n, patches = len(v_shards), normed.shape[0] // frames
    rows = patches // CHUNKS
    frame = pl.BlockSpec((patches, WIDTH), lambda f: (f, 0))
    return pl.pallas_call(
        partial(space_rest_kernel, n),
        grid=(frames,),
        in_specs=[frame, frame, WHOLE] + shard_specs(n) * 2 + [HBM],
        out_specs=[frame, frame, pl.BlockSpec((None, rows, WIDTH), lambda f: (f, 0, 0)), TOKEN_SPEC],
        out_shape=[jax.ShapeDtypeStruct(normed.shape, BF16)] * 2
        + [jax.ShapeDtypeStruct((frames, rows, WIDTH), BF16), TOKEN],
        scratch_shapes=[pltpu.VMEM((WIDTH, WIDTH), BF16)] * 2
        + [pltpu.VMEM((rows, WIDTH), BF16), pltpu.VMEM((patches, WIDTH), BF16)]
        + [pltpu.SemaphoreType.DMA((NEAR,))] * 2,
        compiler_params=params(28),
        cost_estimate=cost(frames * patches, WIDTH, 2 * WIDTH),
        name="space_rest",
    )(normed, first, picks, *second_shards, *v_shards, token)


def space_attend(chunk, frames, first, second, v, picks, token):
    patches = v.shape[0] // frames
    rows = patches // CHUNKS
    frame = pl.BlockSpec((patches, WIDTH), lambda f: (f, 0))
    return pl.pallas_call(
        partial(space_attend_kernel, chunk * rows),
        grid=(frames,),
        in_specs=[frame, frame, frame, WHOLE, HBM],
        out_specs=pl.BlockSpec((None, rows, WIDTH), lambda f: (f, 0, 0)),
        out_shape=jax.ShapeDtypeStruct((frames, rows, WIDTH), BF16),
        scratch_shapes=[pltpu.VMEM((rows, WIDTH), BF16), pltpu.VMEM((patches, WIDTH), BF16)],
        compiler_params=params(18),
        cost_estimate=cost(frames * rows, WIDTH, WIDTH),
        name=f"space_attend_{chunk}",
    )(first, second, v, picks, token)


def space_out(chunk, peers, attended, clips, shards_of):
    frames, rows, n = attended.shape[0], attended.shape[1], len(shards_of)
    each = rows // peers
    direct = each % 16 == 0
    if direct:
        out_spec = pl.BlockSpec((peers, 1, each, WIDTH), lambda f: (0, f, 0, 0))
        shape = (peers, frames, each, WIDTH)
    else:
        out_spec = pl.BlockSpec((None, rows, WIDTH), lambda f: (f, 0, 0))
        shape = (frames, rows, WIDTH)
    hidden, token = pl.pallas_call(
        partial(space_out_kernel, n),
        grid=(frames,),
        in_specs=[
            pl.BlockSpec((None, rows, WIDTH), lambda f: (f, 0, 0)),
            pl.BlockSpec((None, rows, WIDTH), lambda f: (f, chunk, 0)),
        ]
        + shard_specs(n),
        out_specs=[out_spec, TOKEN_SPEC],
        out_shape=[jax.ShapeDtypeStruct(shape, BF16), TOKEN],
        scratch_shapes=[pltpu.VMEM((WIDTH, WIDTH), BF16), pltpu.SemaphoreType.DMA((NEAR,))],
        compiler_params=params(12),
        cost_estimate=cost(frames * rows, WIDTH, WIDTH),
        name=f"space_out_{chunk}",
    )(attended, clips, *shards_of)
    if not direct:
        hidden = jnp.swapaxes(hidden.reshape(frames, peers, each, WIDTH), 0, 1)
    return hidden, token


def time_attend(chunk, moved, patches_here, picks, shards_of, token):
    rows, n = moved.shape[0], len(shards_of)
    return pl.pallas_call(
        partial(time_kernel, n, patches_here),
        in_specs=[WHOLE, WHOLE] + [HBM] * (n + 1),
        out_specs=[WHOLE, WHOLE],
        out_shape=[jax.ShapeDtypeStruct((rows, WIDTH), BF16), TOKEN],
        scratch_shapes=[pltpu.VMEM((3, WIDTH, WIDTH), BF16)]
        + [pltpu.VMEM((rows, WIDTH), BF16)] * 3
        + [pltpu.SemaphoreType.DMA((3, n))],
        compiler_params=params(52),
        cost_estimate=cost(rows, WIDTH, 4 * WIDTH),
        name=f"time_attend_{chunk}",
    )(moved, picks, *shards_of, token)


def time_out(chunk, attended, moved, shards_of, token):
    rows, n = moved.shape[0], len(shards_of)
    return pl.pallas_call(
        partial(time_out_kernel, n),
        in_specs=[WHOLE, WHOLE] + shard_specs(n) + [HBM],
        out_specs=[WHOLE, WHOLE],
        out_shape=[jax.ShapeDtypeStruct((rows, WIDTH), BF16), TOKEN],
        scratch_shapes=[pltpu.VMEM((WIDTH, WIDTH), BF16), pltpu.SemaphoreType.DMA((NEAR,))],
        compiler_params=params(16),
        cost_estimate=cost(rows, WIDTH, WIDTH),
        name=f"time_out_{chunk}",
    )(attended, moved, *shards_of, token)


def swap(value, mask, axis="dp"):
    return lax.ppermute(value, axis, [(i, i ^ mask) for i in range(lax.axis_size(axis))])


def after(value, other):
    return pl.pallas_call(
        lambda *refs: None,
        in_specs=[HBM] * 2,
        out_specs=HBM,
        out_shape=jax.ShapeDtypeStruct(value.shape, value.dtype),
        input_output_aliases={0: 0},
        compiler_params=params(1),
        name="after",
    )(value, other)


def together(*values):
    n = len(values)
    return pl.pallas_call(
        lambda *refs: None,
        in_specs=[HBM] * n,
        out_specs=[HBM] * n,
        out_shape=[jax.ShapeDtypeStruct(value.shape, value.dtype) for value in values],
        input_output_aliases={i: i for i in range(n)},
        compiler_params=params(1),
        name="together",
    )(*values)


def shards(clips, w_space_qkv, w_space_out, w_time_qkv, w_time_out, space_pattern, time_pattern):
    peers = lax.axis_size("tm")
    frames, patches = clips.shape[1], clips.shape[2]
    frames_all = frames * peers
    each = patches // CHUNKS // peers
    local = clips.reshape(frames, patches, WIDTH)
    space_picks, time_picks = space_pattern.T, time_pattern.T

    part = lax.axis_index("tm") & 1
    first_there = swap(lax.dynamic_slice_in_dim(w_space_qkv, part * WIDTH, WIDTH, 1), 2)
    own_mate = swap(w_space_qkv, 1)
    own = [w_space_qkv, own_mate]
    normed, token = norm_rows(local.reshape(frames * patches, WIDTH))
    first_there, token = together(first_there, token)
    first_mate = swap(first_there, 1)
    second_there = swap(first_there, 1, "tm")
    v_there = swap(w_space_qkv[:, 2 * WIDTH :], 2)
    out_there = swap(w_space_out, 2)
    (token,) = together(token)
    first, token = space_first(normed, own + [first_there, first_mate], token)
    second_there, v_there, token = together(second_there, v_there, token)
    second_mate, v_mate = swap(second_there, 1), swap(v_there, 1)
    (token,) = together(token)
    second, v, attended, token = space_rest(
        frames, normed, first, own + [second_there, second_mate], own + [v_there, v_mate], space_picks, token
    )
    out_there, token = together(out_there, token)
    space_out_shards = [w_space_out, swap(w_space_out, 1), out_there, swap(out_there, 1)]
    moved = []
    for chunk in range(CHUNKS):
        if chunk > 0:
            attended = space_attend(chunk, frames, first, second, v, space_picks, token)
        hidden, token = space_out(chunk, peers, attended, local, space_out_shards)
        moved.append(lax.all_to_all(hidden, "tm", split_axis=0, concat_axis=0, tiled=True))
    qkv_there = swap(w_time_qkv, 2)
    qkv_there, token = together(qkv_there, token)
    time_qkv = [w_time_qkv, swap(w_time_qkv, 1), qkv_there, swap(qkv_there, 1)]
    time_there = swap(w_time_out, 2)
    returned = []
    for chunk in range(CHUNKS):
        rows = moved[chunk].reshape(frames_all * each, WIDTH)
        attended, token = time_attend(chunk, rows, each, time_picks, time_qkv, token)
        if chunk == 0:
            time_there, token = together(time_there, token)
            time_shards = [w_time_out, swap(w_time_out, 1), time_there, swap(time_there, 1)]
        finished, token = time_out(chunk, attended, rows, time_shards, token)
        finished = finished.reshape(peers, frames, each, WIDTH)
        if chunk > 0:
            finished = after(finished, back)
        back = lax.all_to_all(finished, "tm", split_axis=0, concat_axis=0, tiled=True)
        returned.append(jnp.swapaxes(back, 0, 1).reshape(frames, patches // CHUNKS, WIDTH))
    return jnp.concatenate(returned, axis=1)[None]


def solution(mesh):
    return jax.shard_map(
        shards,
        mesh=mesh,
        in_specs=(
            P("dp", "tm", None, None),
            P("dp", None),
            P("dp", None),
            P("dp", None),
            P("dp", None),
            P(),
            P(),
        ),
        out_specs=P("dp", "tm", None, None),
        check_vma=False,
    )
```

```python
from functools import partial

import jax
import jax.numpy as jnp
from jax import lax
from jax.experimental import pallas as pl
from jax.experimental.pallas import tpu as pltpu
from jax.sharding import PartitionSpec as P

HEADS = 16
HEAD_FEATURES = 72
WIDTH = 1152
CHUNKS = 2
NEAR = 2
LANES = 128
MIB = 1024 * 1024
QUERY_SCALE = HEAD_FEATURES**-0.5 * 1.4426950408889634

F32 = jnp.float32
BF16 = jnp.bfloat16


def dot(left, right):
    return jnp.dot(left, right, preferred_element_type=F32)


def dot_rows(left, right):
    return lax.dot_general(left, right, (((1,), (1,)), ((), ())), preferred_element_type=F32)


def layer_norm(values):
    average = jnp.mean(values, axis=-1, keepdims=True)
    centred = values - average
    variance = jnp.mean(centred * centred, axis=-1, keepdims=True)
    return centred * lax.rsqrt(variance + 1e-06)


def iota(shape, dim):
    return lax.broadcasted_iota(jnp.int32, shape, dim)


def head_gather():
    feature, column = iota((WIDTH, LANES), 0), iota((WIDTH, LANES), 1)
    head = jnp.where(column >= HEADS, column - HEADS, column)
    start = head * HEAD_FEATURES
    inside = (feature >= start) & (feature < start + HEAD_FEATURES) & (column < 2 * HEADS)
    return jnp.where(inside, 1.0, 0.0).astype(BF16)


def head_spread():
    column, feature = iota((LANES, WIDTH), 0), iota((LANES, WIDTH), 1)
    head = jnp.where(column >= HEADS, column - HEADS, column)
    start = head * HEAD_FEATURES
    inside = (feature >= start) & (feature < start + HEAD_FEATURES) & (column < 2 * HEADS)
    return jnp.where(inside, 1.0, 0.0).astype(BF16)


def head_norm(packed, gather, spread, scale):
    values = packed.astype(F32)
    squares = dot((values * values).astype(BF16), gather) * (1.0 / HEAD_FEATURES)
    factor = lax.rsqrt(squares + 1e-06) * scale
    high = factor.astype(BF16)
    low = (factor - high.astype(F32)).astype(BF16)
    column = iota(factor.shape, 1)
    both = jnp.where(column < HEADS, high.astype(F32), jnp.where(column < 2 * HEADS, low.astype(F32), 0.0))
    return (values * dot(both.astype(BF16), spread)).astype(BF16)


def block_table(picks):
    blocks = picks.shape[1]
    row = iota((blocks, blocks), 0)
    hits = row == picks[0:1]
    for pick in range(1, picks.shape[0]):
        hits = hits | (row == picks[pick : pick + 1])
    return jnp.where(hits, 1.0, 0.0)


def block_mask(table, query_block, key_block):
    blocks = table.shape[0]
    queries, keys = query_block.shape[0], key_block.shape[0]
    query_hot = jnp.where(query_block == iota((queries, blocks), 1), 1.0, 0.0)
    key_hot = jnp.where(key_block == iota((keys, blocks), 1), 1.0, 0.0)
    return dot_rows(dot_rows(query_hot, table), key_hot)


def shift_of(size):
    assert size & (size - 1) == 0
    return size.bit_length() - 1


def head_window(head):
    first = head * HEAD_FEATURES
    tile = first // LANES
    width = LANES if (first + HEAD_FEATURES - 1) // LANES == tile else 2 * LANES
    return tile * LANES, width, first - tile * LANES


def attend(query_of, key_of, value_of, mask, store):
    for head in range(HEADS):
        start, width, offset = head_window(head)
        window = slice(start, start + width)
        keys, values = key_of(window), value_of(window)
        lane = iota((1, width), 1)
        inside = (lane >= offset) & (lane < offset + HEAD_FEATURES)
        spare = 0 if offset > 0 else HEAD_FEATURES
        marks = jnp.where(inside, 1.0, 0.0).astype(BF16)
        ones = jnp.where(lane == spare, 1.0, 0.0).astype(BF16)
        scores = dot_rows(query_of(window), keys * marks)
        weights = jnp.exp2(scores).astype(BF16) * mask
        blended = dot(weights, values * marks + ones)
        blended = blended * (1.0 / blended[:, spare : spare + 1])
        store(window, inside, blended.astype(BF16))


def merge(ref, row, window, inside, blended):
    old = ref[row, window]
    ref[row, window] = jnp.where(jnp.broadcast_to(inside, blended.shape), blended, old)


def lay_shards(refs, near, column, weight, sem):
    me = lax.axis_index("dp")
    rows, width = refs[0].shape[0], weight.shape[1]
    copies = []
    for k, ref in enumerate(refs):
        place = weight.at[pl.ds(pl.multiple_of(jnp.bitwise_xor(me, k) * rows, 16), rows), :]
        if k < near:
            source = ref if ref.shape[1] == width else ref.at[:, pl.ds(column, width)]
            copies.append(pltpu.make_async_copy(source, place, sem.at[k]))
            copies[-1].start()
        else:
            place[...] = ref[...]
    return copies


def wait_all(copies):
    for copy in copies:
        copy.wait()


def norm_kernel(x_ref, out_ref, token_ref):
    out_ref[...] = layer_norm(x_ref[...].astype(F32)).astype(BF16)
    token_ref[...] = jnp.zeros_like(token_ref)


def part_scale(part):
    return jnp.where(part == 0, QUERY_SCALE, 1.0).astype(F32)


def space_first_kernel(n, normed_ref, *refs):
    w_refs, (_, out_ref, token_ref, weight, sem) = refs[:n], refs[n:]
    part = lax.axis_index("tm") & 1

    @pl.when(pl.program_id(0) == 0)
    def _():
        wait_all(lay_shards(w_refs, NEAR, pl.multiple_of(part * WIDTH, LANES), weight, sem))
        token_ref[...] = jnp.zeros_like(token_ref)

    packed = dot(normed_ref[...], weight[...]).astype(BF16)
    out_ref[...] = head_norm(packed, head_gather(), head_spread(), part_scale(part))


def pick_queries(part, first_ref, second_ref, queries, q_s, k_s):
    @pl.when(part == 0)
    def _():
        q_s[...] = first_ref[queries, :]
        k_s[...] = second_ref[...]

    @pl.when(part == 1)
    def _():
        q_s[...] = second_ref[queries, :]
        k_s[...] = first_ref[...]


def space_blocks(first_row, picks, v_ref, out_ref, q_s, k_s):
    rows, patches = q_s.shape[0], k_s.shape[0]
    shift = shift_of(patches // picks.shape[1])
    query_block = (iota((rows, 1), 0) + first_row) >> shift
    key_block = iota((patches, 1), 0) >> shift
    mask = block_mask(block_table(picks), query_block, key_block).astype(BF16)
    attend(
        lambda window: q_s[:, window],
        lambda window: k_s[:, window],
        lambda window: v_ref[:, window],
        mask,
        lambda window, inside, blended: merge(out_ref, slice(0, rows), window, inside, blended),
    )


def space_rest_kernel(n, normed_ref, first_ref, picks_ref, *refs):
    second_refs, v_refs, refs = refs[:n], refs[n : 2 * n], refs[2 * n :]
    _, second_ref, v_ref, out_ref, token_ref, weight, v_weight, q_s, k_s, sem, v_sem = refs
    part = lax.axis_index("tm") & 1

    @pl.when(pl.program_id(0) == 0)
    def _():
        copies = lay_shards(v_refs, NEAR, 2 * WIDTH, v_weight, v_sem)
        copies += lay_shards(second_refs, NEAR, pl.multiple_of((1 - part) * WIDTH, LANES), weight, sem)
        wait_all(copies)
        token_ref[...] = jnp.zeros_like(token_ref)

    normed = normed_ref[...]
    v_ref[...] = dot(normed, v_weight[...]).astype(BF16)
    packed = dot(normed, weight[...]).astype(BF16)
    second_ref[...] = head_norm(packed, head_gather(), head_spread(), part_scale(1 - part))
    pick_queries(part, first_ref, second_ref, pl.ds(0, q_s.shape[0]), q_s, k_s)
    space_blocks(0, picks_ref[...], v_ref, out_ref, q_s, k_s)


def space_attend_kernel(first_row, first_ref, second_ref, v_ref, picks_ref, _, out_ref, q_s, k_s):
    part = lax.axis_index("tm") & 1
    pick_queries(part, first_ref, second_ref, pl.ds(first_row, q_s.shape[0]), q_s, k_s)
    space_blocks(first_row, picks_ref[...], v_ref, out_ref, q_s, k_s)


def space_out_kernel(n, attended_ref, x_ref, *refs):
    w_refs, (hidden_ref, token_ref, weight, sem) = refs[:n], refs[n:]

    @pl.when(pl.program_id(0) == 0)
    def _():
        wait_all(lay_shards(w_refs, NEAR, 0, weight, sem))
        token_ref[...] = jnp.zeros_like(token_ref)

    branch = dot(attended_ref[...], weight[...])
    hidden = (x_ref[...].astype(F32) + branch).astype(BF16)
    hidden_ref[...] = hidden.reshape(hidden_ref.shape)


def time_kernel(n, patches_here, x_ref, picks_ref, *refs):
    w_refs, (_, attended, token_ref, weight, q_s, k_s, v_s, sem) = refs[:n], refs[n:]
    token_ref[...] = jnp.zeros_like(token_ref)
    copies = [
        lay_shards(w_refs, n, part * WIDTH, weight.at[part], sem.at[part]) for part in range(3)
    ]
    rows = x_ref.shape[0]
    frames = rows // patches_here
    tile_patches = 16 if patches_here % 16 == 0 else patches_here
    tile = tile_patches * frames
    pattern = picks_ref[...]
    shift = shift_of(tile_patches)
    block_shift = shift_of(frames // pattern.shape[1]) + shift
    block = iota((tile, 1), 0) >> block_shift
    allowed = block_mask(block_table(pattern), block, block)
    same = (iota((tile, tile), 0) & (tile_patches - 1)) == (iota((tile, tile), 1) & (tile_patches - 1))
    mask = jnp.where(same, allowed, 0.0).astype(BF16)
    gather, spread = head_gather(), head_spread()
    normed = layer_norm(x_ref[...].astype(F32)).astype(BF16)
    wait_all(copies[0])
    q_s[...] = head_norm(dot(normed, weight[0]).astype(BF16), gather, spread, QUERY_SCALE)
    wait_all(copies[1])
    k_s[...] = head_norm(dot(normed, weight[1]).astype(BF16), gather, spread, 1.0)
    wait_all(copies[2])
    v_s[...] = dot(normed, weight[2]).astype(BF16)

    for first in range(0, patches_here, tile_patches):

        def rows_of(ref, window):
            if tile_patches == patches_here:
                return ref[:, window]
            return jnp.concatenate(
                [ref[pl.ds(f * patches_here + first, tile_patches), window] for f in range(frames)], axis=0
            )

        def store(window, inside, blended):
            if tile_patches == patches_here:
                merge(attended, slice(0, rows), window, inside, blended)
                return
            for f in range(frames):
                merge(
                    attended,
                    pl.ds(f * patches_here + first, tile_patches),
                    window,
                    inside,
                    blended[f * tile_patches : (f + 1) * tile_patches],
                )

        attend(
            partial(rows_of, q_s), partial(rows_of, k_s), partial(rows_of, v_s), mask, store
        )


def time_out_kernel(n, attended_ref, x_ref, *refs):
    w_refs, (_, out_ref, token_ref, weight, sem) = refs[:n], refs[n:]
    wait_all(lay_shards(w_refs, NEAR, 0, weight, sem))
    token_ref[...] = jnp.zeros_like(token_ref)
    out_ref[...] = (x_ref[...].astype(F32) + dot(attended_ref[...], weight[...])).astype(BF16)


HBM = pl.BlockSpec(memory_space=pl.ANY)
WHOLE = pl.BlockSpec(memory_space=pltpu.VMEM)
TOKEN = jax.ShapeDtypeStruct((8, LANES), F32)
TOKEN_SPEC = pl.BlockSpec((8, LANES), lambda *_: (0, 0))


def params(mib):
    return pltpu.CompilerParams(vmem_limit_bytes=mib * MIB)


def cost(rows, depth, columns, extra=0):
    return pl.CostEstimate(flops=rows * depth * columns // 8, bytes_accessed=2 * rows * columns // 8, transcendentals=0)


def norm_rows(rows_in):
    rows, step = rows_in.shape[0], 256
    spec = pl.BlockSpec((step, WIDTH), lambda i: (i, 0))
    return pl.pallas_call(
        norm_kernel,
        grid=(rows // step,),
        in_specs=[spec],
        out_specs=[spec, TOKEN_SPEC],
        out_shape=[jax.ShapeDtypeStruct((rows, WIDTH), BF16), TOKEN],
        compiler_params=params(10),
        name="norm_rows",
    )(rows_in)


def shard_specs(n):
    return [HBM] * NEAR + [WHOLE] * (n - NEAR)


def space_first(normed, shards_of, token):
    rows, n, step = normed.shape[0], len(shards_of), 256
    flat = pl.BlockSpec((step, WIDTH), lambda i: (i, 0))
    return pl.pallas_call(
        partial(space_first_kernel, n),
        grid=(rows // step,),
        in_specs=[flat] + shard_specs(n) + [HBM],
        out_specs=[flat, TOKEN_SPEC],
        out_shape=[jax.ShapeDtypeStruct((rows, WIDTH), BF16), TOKEN],
        scratch_shapes=[pltpu.VMEM((WIDTH, WIDTH), BF16), pltpu.SemaphoreType.DMA((NEAR,))],
        compiler_params=params(14),
        cost_estimate=cost(rows, WIDTH, WIDTH),
        name="space_first",
    )(normed, *shards_of, token)


def space_rest(frames, normed, first, second_shards, v_shards, picks, token):
    n, patches = len(v_shards), normed.shape[0] // frames
    rows = patches // CHUNKS
    frame = pl.BlockSpec((patches, WIDTH), lambda f: (f, 0))
    return pl.pallas_call(
        partial(space_rest_kernel, n),
        grid=(frames,),
        in_specs=[frame, frame, WHOLE] + shard_specs(n) * 2 + [HBM],
        out_specs=[frame, frame, pl.BlockSpec((None, rows, WIDTH), lambda f: (f, 0, 0)), TOKEN_SPEC],
        out_shape=[jax.ShapeDtypeStruct(normed.shape, BF16)] * 2
        + [jax.ShapeDtypeStruct((frames, rows, WIDTH), BF16), TOKEN],
        scratch_shapes=[pltpu.VMEM((WIDTH, WIDTH), BF16)] * 2
        + [pltpu.VMEM((rows, WIDTH), BF16), pltpu.VMEM((patches, WIDTH), BF16)]
        + [pltpu.SemaphoreType.DMA((NEAR,))] * 2,
        compiler_params=params(28),
        cost_estimate=cost(frames * patches, WIDTH, 2 * WIDTH),
        name="space_rest",
    )(normed, first, picks, *second_shards, *v_shards, token)


def space_attend(chunk, frames, first, second, v, picks, token):
    patches = v.shape[0] // frames
    rows = patches // CHUNKS
    frame = pl.BlockSpec((patches, WIDTH), lambda f: (f, 0))
    return pl.pallas_call(
        partial(space_attend_kernel, chunk * rows),
        grid=(frames,),
        in_specs=[frame, frame, frame, WHOLE, HBM],
        out_specs=pl.BlockSpec((None, rows, WIDTH), lambda f: (f, 0, 0)),
        out_shape=jax.ShapeDtypeStruct((frames, rows, WIDTH), BF16),
        scratch_shapes=[pltpu.VMEM((rows, WIDTH), BF16), pltpu.VMEM((patches, WIDTH), BF16)],
        compiler_params=params(18),
        cost_estimate=cost(frames * rows, WIDTH, WIDTH),
        name=f"space_attend_{chunk}",
    )(first, second, v, picks, token)


def space_out(chunk, peers, attended, clips, shards_of):
    frames, rows, n = attended.shape[0], attended.shape[1], len(shards_of)
    each = rows // peers
    direct = each % 16 == 0
    if direct:
        out_spec = pl.BlockSpec((peers, 1, each, WIDTH), lambda f: (0, f, 0, 0))
        shape = (peers, frames, each, WIDTH)
    else:
        out_spec = pl.BlockSpec((None, rows, WIDTH), lambda f: (f, 0, 0))
        shape = (frames, rows, WIDTH)
    hidden, token = pl.pallas_call(
        partial(space_out_kernel, n),
        grid=(frames,),
        in_specs=[
            pl.BlockSpec((None, rows, WIDTH), lambda f: (f, 0, 0)),
            pl.BlockSpec((None, rows, WIDTH), lambda f: (f, chunk, 0)),
        ]
        + shard_specs(n),
        out_specs=[out_spec, TOKEN_SPEC],
        out_shape=[jax.ShapeDtypeStruct(shape, BF16), TOKEN],
        scratch_shapes=[pltpu.VMEM((WIDTH, WIDTH), BF16), pltpu.SemaphoreType.DMA((NEAR,))],
        compiler_params=params(12),
        cost_estimate=cost(frames * rows, WIDTH, WIDTH),
        name=f"space_out_{chunk}",
    )(attended, clips, *shards_of)
    if not direct:
        hidden = jnp.swapaxes(hidden.reshape(frames, peers, each, WIDTH), 0, 1)
    return hidden, token


def time_attend(chunk, moved, patches_here, picks, shards_of, token):
    rows, n = moved.shape[0], len(shards_of)
    return pl.pallas_call(
        partial(time_kernel, n, patches_here),
        in_specs=[WHOLE, WHOLE] + [HBM] * (n + 1),
        out_specs=[WHOLE, WHOLE],
        out_shape=[jax.ShapeDtypeStruct((rows, WIDTH), BF16), TOKEN],
        scratch_shapes=[pltpu.VMEM((3, WIDTH, WIDTH), BF16)]
        + [pltpu.VMEM((rows, WIDTH), BF16)] * 3
        + [pltpu.SemaphoreType.DMA((3, n))],
        compiler_params=params(52),
        cost_estimate=cost(rows, WIDTH, 4 * WIDTH),
        name=f"time_attend_{chunk}",
    )(moved, picks, *shards_of, token)


def time_out(chunk, attended, moved, shards_of, token):
    rows, n = moved.shape[0], len(shards_of)
    return pl.pallas_call(
        partial(time_out_kernel, n),
        in_specs=[WHOLE, WHOLE] + shard_specs(n) + [HBM],
        out_specs=[WHOLE, WHOLE],
        out_shape=[jax.ShapeDtypeStruct((rows, WIDTH), BF16), TOKEN],
        scratch_shapes=[pltpu.VMEM((WIDTH, WIDTH), BF16), pltpu.SemaphoreType.DMA((NEAR,))],
        compiler_params=params(16),
        cost_estimate=cost(rows, WIDTH, WIDTH),
        name=f"time_out_{chunk}",
    )(attended, moved, *shards_of, token)


def swap(value, mask, axis="dp"):
    return lax.ppermute(value, axis, [(i, i ^ mask) for i in range(lax.axis_size(axis))])


def after(value, other):
    return pl.pallas_call(
        lambda *refs: None,
        in_specs=[HBM] * 2,
        out_specs=HBM,
        out_shape=jax.ShapeDtypeStruct(value.shape, value.dtype),
        input_output_aliases={0: 0},
        compiler_params=params(1),
        name="after",
    )(value, other)


def held(value, token):
    probe = token[0, 0]
    return jnp.where(probe != probe, jnp.zeros_like(value), value)


def together(*values):
    n = len(values)
    return pl.pallas_call(
        lambda *refs: None,
        in_specs=[HBM] * n,
        out_specs=[HBM] * n,
        out_shape=[jax.ShapeDtypeStruct(value.shape, value.dtype) for value in values],
        input_output_aliases={i: i for i in range(n)},
        compiler_params=params(1),
        name="together",
    )(*values)


def shards(clips, w_space_qkv, w_space_out, w_time_qkv, w_time_out, space_pattern, time_pattern):
    peers = lax.axis_size("tm")
    frames, patches = clips.shape[1], clips.shape[2]
    frames_all = frames * peers
    each = patches // CHUNKS // peers
    local = clips.reshape(frames, patches, WIDTH)
    space_picks, time_picks = space_pattern.T, time_pattern.T

    part = lax.axis_index("tm") & 1
    first_there = swap(lax.dynamic_slice_in_dim(w_space_qkv, part * WIDTH, WIDTH, 1), 2)
    own_mate = swap(w_space_qkv, 1)
    own = [w_space_qkv, own_mate]
    normed, token = norm_rows(local.reshape(frames * patches, WIDTH))
    first_there, token = together(first_there, token)
    first_mate = swap(first_there, 1)
    second_there = swap(first_there, 1, "tm")
    v_there = swap(w_space_qkv[:, 2 * WIDTH :], 2)
    out_there = swap(w_space_out, 2)
    (token,) = together(token)
    first, token = space_first(normed, own + [first_there, first_mate], token)
    second_there, v_there, token = together(second_there, v_there, token)
    second_mate, v_mate = swap(second_there, 1), swap(v_there, 1)
    (token,) = together(token)
    second, v, attended, token = space_rest(
        frames, normed, first, own + [second_there, second_mate], own + [v_there, v_mate], space_picks, token
    )
    out_there, token = together(out_there, token)
    space_out_shards = [w_space_out, swap(w_space_out, 1), out_there, swap(out_there, 1)]
    moved = []
    for chunk in range(CHUNKS):
        if chunk > 0:
            attended = space_attend(chunk, frames, first, second, v, space_picks, token)
        hidden, token = space_out(chunk, peers, attended, local, space_out_shards)
        moved.append(lax.all_to_all(hidden, "tm", split_axis=0, concat_axis=0, tiled=True))
    qkv_there = swap(w_time_qkv, 2)
    qkv_there, token = together(qkv_there, token)
    time_qkv = [w_time_qkv, swap(w_time_qkv, 1), qkv_there, swap(qkv_there, 1)]
    time_there = swap(w_time_out, 2)
    returned = []
    for chunk in range(CHUNKS):
        rows = moved[chunk].reshape(frames_all * each, WIDTH)
        attended, token = time_attend(chunk, rows, each, time_picks, time_qkv, token)
        if chunk == 0:
            time_there = held(time_there, token)
            time_shards = [w_time_out, swap(w_time_out, 1), time_there, swap(time_there, 1)]
        finished, token = time_out(chunk, attended, rows, time_shards, token)
        finished = finished.reshape(peers, frames, each, WIDTH)
        if chunk > 0:
            finished = after(finished, back)
        back = lax.all_to_all(finished, "tm", split_axis=0, concat_axis=0, tiled=True)
        returned.append(jnp.swapaxes(back, 0, 1).reshape(frames, patches // CHUNKS, WIDTH))
    return jnp.concatenate(returned, axis=1)[None]


def solution(mesh):
    return jax.shard_map(
        shards,
        mesh=mesh,
        in_specs=(
            P("dp", "tm", None, None),
            P("dp", None),
            P("dp", None),
            P("dp", None),
            P("dp", None),
            P(),
            P(),
        ),
        out_specs=P("dp", "tm", None, None),
        check_vma=False,
    )
```

```python
from functools import partial

import jax
import jax.numpy as jnp
from jax import lax
from jax.experimental import pallas as pl
from jax.experimental.pallas import tpu as pltpu
from jax.sharding import PartitionSpec as P

HEADS = 16
HEAD_FEATURES = 72
WIDTH = 1152
CHUNKS = 2
NEAR = 2
LANES = 128
MIB = 1024 * 1024
QUERY_SCALE = HEAD_FEATURES**-0.5 * 1.4426950408889634

F32 = jnp.float32
BF16 = jnp.bfloat16


def dot(left, right):
    return jnp.dot(left, right, preferred_element_type=F32)


def dot_rows(left, right):
    return lax.dot_general(left, right, (((1,), (1,)), ((), ())), preferred_element_type=F32)


def layer_norm(values):
    average = jnp.mean(values, axis=-1, keepdims=True)
    centred = values - average
    variance = jnp.mean(centred * centred, axis=-1, keepdims=True)
    return centred * lax.rsqrt(variance + 1e-06)


def iota(shape, dim):
    return lax.broadcasted_iota(jnp.int32, shape, dim)


def head_gather():
    feature, column = iota((WIDTH, LANES), 0), iota((WIDTH, LANES), 1)
    head = jnp.where(column >= HEADS, column - HEADS, column)
    start = head * HEAD_FEATURES
    inside = (feature >= start) & (feature < start + HEAD_FEATURES) & (column < 2 * HEADS)
    return jnp.where(inside, 1.0, 0.0).astype(BF16)


def head_spread():
    column, feature = iota((LANES, WIDTH), 0), iota((LANES, WIDTH), 1)
    head = jnp.where(column >= HEADS, column - HEADS, column)
    start = head * HEAD_FEATURES
    inside = (feature >= start) & (feature < start + HEAD_FEATURES) & (column < 2 * HEADS)
    return jnp.where(inside, 1.0, 0.0).astype(BF16)


def head_norm(packed, gather, spread, scale):
    values = packed.astype(F32)
    squares = dot((values * values).astype(BF16), gather) * (1.0 / HEAD_FEATURES)
    factor = lax.rsqrt(squares + 1e-06) * scale
    high = factor.astype(BF16)
    low = (factor - high.astype(F32)).astype(BF16)
    column = iota(factor.shape, 1)
    both = jnp.where(column < HEADS, high.astype(F32), jnp.where(column < 2 * HEADS, low.astype(F32), 0.0))
    return (values * dot(both.astype(BF16), spread)).astype(BF16)


def block_table(picks):
    blocks = picks.shape[1]
    row = iota((blocks, blocks), 0)
    hits = row == picks[0:1]
    for pick in range(1, picks.shape[0]):
        hits = hits | (row == picks[pick : pick + 1])
    return jnp.where(hits, 1.0, 0.0)


def block_mask(table, query_block, key_block):
    blocks = table.shape[0]
    queries, keys = query_block.shape[0], key_block.shape[0]
    query_hot = jnp.where(query_block == iota((queries, blocks), 1), 1.0, 0.0)
    key_hot = jnp.where(key_block == iota((keys, blocks), 1), 1.0, 0.0)
    return dot_rows(dot_rows(query_hot, table), key_hot)


def shift_of(size):
    assert size & (size - 1) == 0
    return size.bit_length() - 1


def head_window(head):
    first = head * HEAD_FEATURES
    tile = first // LANES
    width = LANES if (first + HEAD_FEATURES - 1) // LANES == tile else 2 * LANES
    return tile * LANES, width, first - tile * LANES


def attend(query_of, key_of, value_of, mask, store):
    for head in range(HEADS):
        start, width, offset = head_window(head)
        window = slice(start, start + width)
        keys, values = key_of(window), value_of(window)
        lane = iota((1, width), 1)
        inside = (lane >= offset) & (lane < offset + HEAD_FEATURES)
        spare = 0 if offset > 0 else HEAD_FEATURES
        marks = jnp.where(inside, 1.0, 0.0).astype(BF16)
        ones = jnp.where(lane == spare, 1.0, 0.0).astype(BF16)
        scores = dot_rows(query_of(window), keys * marks)
        weights = jnp.exp2(scores).astype(BF16) * mask
        blended = dot(weights, values * marks + ones)
        blended = blended * (1.0 / blended[:, spare : spare + 1])
        store(window, inside, blended.astype(BF16))


def merge(ref, row, window, inside, blended):
    old = ref[row, window]
    ref[row, window] = jnp.where(jnp.broadcast_to(inside, blended.shape), blended, old)


def lay_shards(refs, near, column, weight, sem):
    me = lax.axis_index("dp")
    rows, width = refs[0].shape[0], weight.shape[1]
    copies = []
    for k, ref in enumerate(refs):
        place = weight.at[pl.ds(pl.multiple_of(jnp.bitwise_xor(me, k) * rows, 16), rows), :]
        if k < near:
            source = ref if ref.shape[1] == width else ref.at[:, pl.ds(column, width)]
            copies.append(pltpu.make_async_copy(source, place, sem.at[k]))
            copies[-1].start()
        else:
            place[...] = ref[...]
    return copies


def wait_all(copies):
    for copy in copies:
        copy.wait()


def norm_kernel(x_ref, out_ref, near_ref, far_ref, token_ref):
    normed = layer_norm(x_ref[...].astype(F32)).astype(BF16)
    out_ref[...] = normed
    half = WIDTH // 2
    pair = (lax.axis_index("dp") >> 1) & 1

    @pl.when(pair == 0)
    def _():
        near_ref[...] = normed[:, :half]
        far_ref[...] = normed[:, half:]

    @pl.when(pair == 1)
    def _():
        near_ref[...] = normed[:, half:]
        far_ref[...] = normed[:, :half]

    token_ref[...] = jnp.zeros_like(token_ref)


def half_place(k, rows, weight):
    place = jnp.bitwise_xor(lax.axis_index("dp"), k) & 1
    return weight.at[pl.ds(pl.multiple_of(place * rows, 16), rows), :]


def space_near_kernel(near_ref, own_ref, mate_ref, _, second_ref, v_ref, token_ref, weight, v_weight, sem):
    rows = own_ref.shape[0]
    column = pl.multiple_of((1 - (lax.axis_index("tm") & 1)) * WIDTH, LANES)

    @pl.when(pl.program_id(0) == 0)
    def _():
        copies = []
        for k, ref in enumerate((own_ref, mate_ref)):
            for i, (first, into) in enumerate(((2 * WIDTH, v_weight), (column, weight))):
                source = ref.at[:, pl.ds(first, WIDTH)]
                copies.append(pltpu.make_async_copy(source, half_place(k, rows, into), sem.at[k, i]))
                copies[-1].start()
        wait_all(copies)
        token_ref[...] = jnp.zeros_like(token_ref)

    near = near_ref[...]
    v_ref[...] = dot(near, v_weight[...])
    second_ref[...] = dot(near, weight[...])


def part_scale(part):
    return jnp.where(part == 0, QUERY_SCALE, 1.0).astype(F32)


def space_first_kernel(n, normed_ref, *refs):
    w_refs, (_, out_ref, token_ref, weight, sem) = refs[:n], refs[n:]
    part = lax.axis_index("tm") & 1

    @pl.when(pl.program_id(0) == 0)
    def _():
        wait_all(lay_shards(w_refs, NEAR, pl.multiple_of(part * WIDTH, LANES), weight, sem))
        token_ref[...] = jnp.zeros_like(token_ref)

    packed = dot(normed_ref[...], weight[...]).astype(BF16)
    out_ref[...] = head_norm(packed, head_gather(), head_spread(), part_scale(part))


def pick_queries(part, first_ref, second_ref, queries, q_s, k_s):
    @pl.when(part == 0)
    def _():
        q_s[...] = first_ref[queries, :]
        k_s[...] = second_ref[...]

    @pl.when(part == 1)
    def _():
        q_s[...] = second_ref[queries, :]
        k_s[...] = first_ref[...]


def space_blocks(first_row, picks, v_ref, out_ref, q_s, k_s):
    rows, patches = q_s.shape[0], k_s.shape[0]
    shift = shift_of(patches // picks.shape[1])
    query_block = (iota((rows, 1), 0) + first_row) >> shift
    key_block = iota((patches, 1), 0) >> shift
    mask = block_mask(block_table(picks), query_block, key_block).astype(BF16)
    attend(
        lambda window: q_s[:, window],
        lambda window: k_s[:, window],
        lambda window: v_ref[:, window],
        mask,
        lambda window, inside, blended: merge(out_ref, slice(0, rows), window, inside, blended),
    )


def space_rest_kernel(far_ref, first_ref, second_near, v_near, picks_ref, *refs):
    (second_there, second_mate, v_there, v_mate), refs = refs[:4], refs[4:]
    _, second_ref, v_ref, out_ref, token_ref, weight, v_weight, q_s, k_s = refs
    part = lax.axis_index("tm") & 1

    @pl.when(pl.program_id(0) == 0)
    def _():
        for k, (second, values) in enumerate(((second_there, v_there), (second_mate, v_mate))):
            half_place(k, second.shape[0], weight)[...] = second[...]
            half_place(k, values.shape[0], v_weight)[...] = values[...]
        token_ref[...] = jnp.zeros_like(token_ref)

    far = far_ref[...]
    v_ref[...] = (v_near[...] + dot(far, v_weight[...])).astype(BF16)
    packed = (second_near[...] + dot(far, weight[...])).astype(BF16)
    second_ref[...] = head_norm(packed, head_gather(), head_spread(), part_scale(1 - part))
    pick_queries(part, first_ref, second_ref, pl.ds(0, q_s.shape[0]), q_s, k_s)
    space_blocks(0, picks_ref[...], v_ref, out_ref, q_s, k_s)


def space_attend_kernel(first_row, first_ref, second_ref, v_ref, picks_ref, _, out_ref, q_s, k_s):
    part = lax.axis_index("tm") & 1
    pick_queries(part, first_ref, second_ref, pl.ds(first_row, q_s.shape[0]), q_s, k_s)
    space_blocks(first_row, picks_ref[...], v_ref, out_ref, q_s, k_s)


def space_out_kernel(n, attended_ref, x_ref, *refs):
    w_refs, (hidden_ref, token_ref, weight, sem) = refs[:n], refs[n:]

    @pl.when(pl.program_id(0) == 0)
    def _():
        wait_all(lay_shards(w_refs, NEAR, 0, weight, sem))
        token_ref[...] = jnp.zeros_like(token_ref)

    branch = dot(attended_ref[...], weight[...])
    hidden = (x_ref[...].astype(F32) + branch).astype(BF16)
    hidden_ref[...] = hidden.reshape(hidden_ref.shape)


def time_kernel(n, patches_here, x_ref, picks_ref, *refs):
    w_refs, (_, attended, token_ref, weight, q_s, k_s, v_s, sem) = refs[:n], refs[n:]
    token_ref[...] = jnp.zeros_like(token_ref)
    copies = [
        lay_shards(w_refs, n, part * WIDTH, weight.at[part], sem.at[part]) for part in range(3)
    ]
    rows = x_ref.shape[0]
    frames = rows // patches_here
    tile_patches = 16 if patches_here % 16 == 0 else patches_here
    tile = tile_patches * frames
    pattern = picks_ref[...]
    shift = shift_of(tile_patches)
    block_shift = shift_of(frames // pattern.shape[1]) + shift
    block = iota((tile, 1), 0) >> block_shift
    allowed = block_mask(block_table(pattern), block, block)
    same = (iota((tile, tile), 0) & (tile_patches - 1)) == (iota((tile, tile), 1) & (tile_patches - 1))
    mask = jnp.where(same, allowed, 0.0).astype(BF16)
    gather, spread = head_gather(), head_spread()
    normed = layer_norm(x_ref[...].astype(F32)).astype(BF16)
    wait_all(copies[0])
    q_s[...] = head_norm(dot(normed, weight[0]).astype(BF16), gather, spread, QUERY_SCALE)
    wait_all(copies[1])
    k_s[...] = head_norm(dot(normed, weight[1]).astype(BF16), gather, spread, 1.0)
    wait_all(copies[2])
    v_s[...] = dot(normed, weight[2]).astype(BF16)

    for first in range(0, patches_here, tile_patches):

        def rows_of(ref, window):
            if tile_patches == patches_here:
                return ref[:, window]
            return jnp.concatenate(
                [ref[pl.ds(f * patches_here + first, tile_patches), window] for f in range(frames)], axis=0
            )

        def store(window, inside, blended):
            if tile_patches == patches_here:
                merge(attended, slice(0, rows), window, inside, blended)
                return
            for f in range(frames):
                merge(
                    attended,
                    pl.ds(f * patches_here + first, tile_patches),
                    window,
                    inside,
                    blended[f * tile_patches : (f + 1) * tile_patches],
                )

        attend(
            partial(rows_of, q_s), partial(rows_of, k_s), partial(rows_of, v_s), mask, store
        )


def time_out_kernel(n, attended_ref, x_ref, *refs):
    w_refs, (_, out_ref, token_ref, weight, sem) = refs[:n], refs[n:]
    wait_all(lay_shards(w_refs, NEAR, 0, weight, sem))
    token_ref[...] = jnp.zeros_like(token_ref)
    out_ref[...] = (x_ref[...].astype(F32) + dot(attended_ref[...], weight[...])).astype(BF16)


HBM = pl.BlockSpec(memory_space=pl.ANY)
WHOLE = pl.BlockSpec(memory_space=pltpu.VMEM)
TOKEN = jax.ShapeDtypeStruct((8, LANES), F32)
TOKEN_SPEC = pl.BlockSpec((8, LANES), lambda *_: (0, 0))


def params(mib):
    return pltpu.CompilerParams(vmem_limit_bytes=mib * MIB)


def cost(rows, depth, columns, extra=0):
    return pl.CostEstimate(flops=rows * depth * columns // 8, bytes_accessed=2 * rows * columns // 8, transcendentals=0)


def norm_rows(rows_in):
    rows, step = rows_in.shape[0], 256
    spec = pl.BlockSpec((step, WIDTH), lambda i: (i, 0))
    half = pl.BlockSpec((step, WIDTH // 2), lambda i: (i, 0))
    return pl.pallas_call(
        norm_kernel,
        grid=(rows // step,),
        in_specs=[spec],
        out_specs=[spec, half, half, TOKEN_SPEC],
        out_shape=[jax.ShapeDtypeStruct((rows, WIDTH), BF16)]
        + [jax.ShapeDtypeStruct((rows, WIDTH // 2), BF16)] * 2
        + [TOKEN],
        compiler_params=params(12),
        name="norm_rows",
    )(rows_in)


def space_near(near, own, own_mate, token):
    rows, step = near.shape[0], 256
    flat = pl.BlockSpec((step, WIDTH), lambda i: (i, 0))
    return pl.pallas_call(
        space_near_kernel,
        grid=(rows // step,),
        in_specs=[pl.BlockSpec((step, WIDTH // 2), lambda i: (i, 0)), HBM, HBM, HBM],
        out_specs=[flat, flat, TOKEN_SPEC],
        out_shape=[jax.ShapeDtypeStruct((rows, WIDTH), F32)] * 2 + [TOKEN],
        scratch_shapes=[pltpu.VMEM((WIDTH // 2, WIDTH), BF16)] * 2 + [pltpu.SemaphoreType.DMA((2, 2))],
        compiler_params=params(14),
        cost_estimate=cost(rows, WIDTH, WIDTH),
        name="space_near",
    )(near, own, own_mate, token)


def shard_specs(n):
    return [HBM] * NEAR + [WHOLE] * (n - NEAR)


def space_first(normed, shards_of, token):
    rows, n, step = normed.shape[0], len(shards_of), 256
    flat = pl.BlockSpec((step, WIDTH), lambda i: (i, 0))
    return pl.pallas_call(
        partial(space_first_kernel, n),
        grid=(rows // step,),
        in_specs=[flat] + shard_specs(n) + [HBM],
        out_specs=[flat, TOKEN_SPEC],
        out_shape=[jax.ShapeDtypeStruct((rows, WIDTH), BF16), TOKEN],
        scratch_shapes=[pltpu.VMEM((WIDTH, WIDTH), BF16), pltpu.SemaphoreType.DMA((NEAR,))],
        compiler_params=params(14),
        cost_estimate=cost(rows, WIDTH, WIDTH),
        name="space_first",
    )(normed, *shards_of, token)


def space_rest(frames, far, first, second_near, v_near, second_shards, v_shards, picks, token):
    patches = far.shape[0] // frames
    rows = patches // CHUNKS
    frame = pl.BlockSpec((patches, WIDTH), lambda f: (f, 0))
    return pl.pallas_call(
        space_rest_kernel,
        grid=(frames,),
        in_specs=[pl.BlockSpec((patches, WIDTH // 2), lambda f: (f, 0)), frame, frame, frame] + [WHOLE] * 5 + [HBM],
        out_specs=[frame, frame, pl.BlockSpec((None, rows, WIDTH), lambda f: (f, 0, 0)), TOKEN_SPEC],
        out_shape=[jax.ShapeDtypeStruct(first.shape, BF16)] * 2
        + [jax.ShapeDtypeStruct((frames, rows, WIDTH), BF16), TOKEN],
        scratch_shapes=[pltpu.VMEM((WIDTH // 2, WIDTH), BF16)] * 2
        + [pltpu.VMEM((rows, WIDTH), BF16), pltpu.VMEM((patches, WIDTH), BF16)],
        compiler_params=params(32),
        cost_estimate=cost(frames * patches, WIDTH, 2 * WIDTH),
        name="space_rest",
    )(far, first, second_near, v_near, picks, *second_shards, *v_shards, token)


def space_attend(chunk, frames, first, second, v, picks, token):
    patches = v.shape[0] // frames
    rows = patches // CHUNKS
    frame = pl.BlockSpec((patches, WIDTH), lambda f: (f, 0))
    return pl.pallas_call(
        partial(space_attend_kernel, chunk * rows),
        grid=(frames,),
        in_specs=[frame, frame, frame, WHOLE, HBM],
        out_specs=pl.BlockSpec((None, rows, WIDTH), lambda f: (f, 0, 0)),
        out_shape=jax.ShapeDtypeStruct((frames, rows, WIDTH), BF16),
        scratch_shapes=[pltpu.VMEM((rows, WIDTH), BF16), pltpu.VMEM((patches, WIDTH), BF16)],
        compiler_params=params(18),
        cost_estimate=cost(frames * rows, WIDTH, WIDTH),
        name=f"space_attend_{chunk}",
    )(first, second, v, picks, token)


def space_out(chunk, peers, attended, clips, shards_of):
    frames, rows, n = attended.shape[0], attended.shape[1], len(shards_of)
    each = rows // peers
    direct = each % 16 == 0
    if direct:
        out_spec = pl.BlockSpec((peers, 1, each, WIDTH), lambda f: (0, f, 0, 0))
        shape = (peers, frames, each, WIDTH)
    else:
        out_spec = pl.BlockSpec((None, rows, WIDTH), lambda f: (f, 0, 0))
        shape = (frames, rows, WIDTH)
    hidden, token = pl.pallas_call(
        partial(space_out_kernel, n),
        grid=(frames,),
        in_specs=[
            pl.BlockSpec((None, rows, WIDTH), lambda f: (f, 0, 0)),
            pl.BlockSpec((None, rows, WIDTH), lambda f: (f, chunk, 0)),
        ]
        + shard_specs(n),
        out_specs=[out_spec, TOKEN_SPEC],
        out_shape=[jax.ShapeDtypeStruct(shape, BF16), TOKEN],
        scratch_shapes=[pltpu.VMEM((WIDTH, WIDTH), BF16), pltpu.SemaphoreType.DMA((NEAR,))],
        compiler_params=params(12),
        cost_estimate=cost(frames * rows, WIDTH, WIDTH),
        name=f"space_out_{chunk}",
    )(attended, clips, *shards_of)
    if not direct:
        hidden = jnp.swapaxes(hidden.reshape(frames, peers, each, WIDTH), 0, 1)
    return hidden, token


def time_attend(chunk, moved, patches_here, picks, shards_of, token):
    rows, n = moved.shape[0], len(shards_of)
    return pl.pallas_call(
        partial(time_kernel, n, patches_here),
        in_specs=[WHOLE, WHOLE] + [HBM] * (n + 1),
        out_specs=[WHOLE, WHOLE],
        out_shape=[jax.ShapeDtypeStruct((rows, WIDTH), BF16), TOKEN],
        scratch_shapes=[pltpu.VMEM((3, WIDTH, WIDTH), BF16)]
        + [pltpu.VMEM((rows, WIDTH), BF16)] * 3
        + [pltpu.SemaphoreType.DMA((3, n))],
        compiler_params=params(52),
        cost_estimate=cost(rows, WIDTH, 4 * WIDTH),
        name=f"time_attend_{chunk}",
    )(moved, picks, *shards_of, token)


def time_out(chunk, attended, moved, shards_of, token):
    rows, n = moved.shape[0], len(shards_of)
    return pl.pallas_call(
        partial(time_out_kernel, n),
        in_specs=[WHOLE, WHOLE] + shard_specs(n) + [HBM],
        out_specs=[WHOLE, WHOLE],
        out_shape=[jax.ShapeDtypeStruct((rows, WIDTH), BF16), TOKEN],
        scratch_shapes=[pltpu.VMEM((WIDTH, WIDTH), BF16), pltpu.SemaphoreType.DMA((NEAR,))],
        compiler_params=params(16),
        cost_estimate=cost(rows, WIDTH, WIDTH),
        name=f"time_out_{chunk}",
    )(attended, moved, *shards_of, token)


def place_kernel(back_ref, *refs):
    out_ref = refs[-1]
    out_ref[...] = back_ref[...].reshape(out_ref.shape)


def place(chunk, back, patches, into):
    peers, frames, each, _ = back.shape
    rows = peers * each
    return pl.pallas_call(
        place_kernel,
        grid=(frames,),
        in_specs=[pl.BlockSpec((peers, None, each, WIDTH), lambda f: (0, f, 0, 0))] + [HBM] * len(into),
        out_specs=pl.BlockSpec((None, rows, WIDTH), lambda f: (f, chunk, 0)),
        out_shape=jax.ShapeDtypeStruct((frames, patches, WIDTH), BF16),
        input_output_aliases={1: 0} if into else {},
        compiler_params=params(8),
        name=f"place_{chunk}",
    )(back, *into)


def swap(value, mask, axis="dp"):
    return lax.ppermute(value, axis, [(i, i ^ mask) for i in range(lax.axis_size(axis))])


def after(value, other):
    return pl.pallas_call(
        lambda *refs: None,
        in_specs=[HBM] * 2,
        out_specs=HBM,
        out_shape=jax.ShapeDtypeStruct(value.shape, value.dtype),
        input_output_aliases={0: 0},
        compiler_params=params(1),
        name="after",
    )(value, other)


def part_kernel(w_ref, out_ref, sem):
    column = pl.multiple_of((lax.axis_index("tm") & 1) * WIDTH, LANES)
    copy = pltpu.make_async_copy(w_ref.at[:, pl.ds(column, WIDTH)], out_ref, sem)
    copy.start()
    copy.wait()


def part_columns(weight):
    return pl.pallas_call(
        part_kernel,
        in_specs=[HBM],
        out_specs=WHOLE,
        out_shape=jax.ShapeDtypeStruct((weight.shape[0], WIDTH), BF16),
        scratch_shapes=[pltpu.SemaphoreType.DMA],
        compiler_params=params(4),
        name="part_columns",
    )(weight)


def held(value, token):
    probe = token[0, 0]
    return jnp.where(probe != probe, jnp.zeros_like(value), value)


def together(*values):
    n = len(values)
    return pl.pallas_call(
        lambda *refs: None,
        in_specs=[HBM] * n,
        out_specs=[HBM] * n,
        out_shape=[jax.ShapeDtypeStruct(value.shape, value.dtype) for value in values],
        input_output_aliases={i: i for i in range(n)},
        compiler_params=params(1),
        name="together",
    )(*values)


def shards(clips, w_space_qkv, w_space_out, w_time_qkv, w_time_out, space_pattern, time_pattern):
    peers = lax.axis_size("tm")
    frames, patches = clips.shape[1], clips.shape[2]
    frames_all = frames * peers
    each = patches // CHUNKS // peers
    local = clips.reshape(frames, patches, WIDTH)
    space_picks, time_picks = space_pattern.T, time_pattern.T

    first_there = swap(part_columns(w_space_qkv), 2)
    own_mate = swap(w_space_qkv, 1)
    own = [w_space_qkv, own_mate]
    normed, near, far, token = norm_rows(local.reshape(frames * patches, WIDTH))
    second_near, v_near, token = space_near(near, w_space_qkv, own_mate, token)
    first_there, token = together(first_there, token)
    first_mate = swap(first_there, 1)
    second_there = swap(first_there, 1, "tm")
    v_there = swap(w_space_qkv[:, 2 * WIDTH :], 2)
    out_there = swap(w_space_out, 2)
    (token,) = together(token)
    first, token = space_first(normed, own + [first_there, first_mate], token)
    second_there, v_there, token = together(second_there, v_there, token)
    second_mate, v_mate = swap(second_there, 1), swap(v_there, 1)
    (token,) = together(token)
    second, v, attended, token = space_rest(
        frames, far, first, second_near, v_near, [second_there, second_mate], [v_there, v_mate], space_picks, token
    )
    out_there, token = together(out_there, token)
    space_out_shards = [w_space_out, swap(w_space_out, 1), out_there, swap(out_there, 1)]
    moved = []
    for chunk in range(CHUNKS):
        if chunk > 0:
            attended = space_attend(chunk, frames, first, second, v, space_picks, token)
        hidden, token = space_out(chunk, peers, attended, local, space_out_shards)
        moved.append(lax.all_to_all(hidden, "tm", split_axis=0, concat_axis=0, tiled=True))
    qkv_there = swap(w_time_qkv, 2)
    qkv_there, token = together(qkv_there, token)
    time_qkv = [w_time_qkv, swap(w_time_qkv, 1), qkv_there, swap(qkv_there, 1)]
    time_there = swap(w_time_out, 2)
    returned = []
    for chunk in range(CHUNKS):
        rows = moved[chunk].reshape(frames_all * each, WIDTH)
        attended, token = time_attend(chunk, rows, each, time_picks, time_qkv, token)
        if chunk == 0:
            time_there = held(time_there, token)
            time_shards = [w_time_out, swap(w_time_out, 1), time_there, swap(time_there, 1)]
        finished, token = time_out(chunk, attended, rows, time_shards, token)
        finished = finished.reshape(peers, frames, each, WIDTH)
        if chunk > 0:
            finished = after(finished, back)
        back = lax.all_to_all(finished, "tm", split_axis=0, concat_axis=0, tiled=True)
        if each % 16 == 0:
            returned = [place(chunk, back, patches, returned)]
        else:
            returned.append(jnp.swapaxes(back, 0, 1).reshape(frames, patches // CHUNKS, WIDTH))
    return (returned[0] if len(returned) == 1 else jnp.concatenate(returned, axis=1))[None]


def solution(mesh):
    return jax.shard_map(
        shards,
        mesh=mesh,
        in_specs=(
            P("dp", "tm", None, None),
            P("dp", None),
            P("dp", None),
            P("dp", None),
            P("dp", None),
            P(),
            P(),
        ),
        out_specs=P("dp", "tm", None, None),
        check_vma=False,
    )
```

```python
from functools import partial

import jax
import jax.numpy as jnp
from jax import lax
from jax.experimental import pallas as pl
from jax.experimental.pallas import tpu as pltpu
from jax.sharding import PartitionSpec as P

HEADS = 16
HEAD_FEATURES = 72
WIDTH = 1152
CHUNKS = 2
NEAR = 2
LANES = 128
MIB = 1024 * 1024
QUERY_SCALE = HEAD_FEATURES**-0.5 * 1.4426950408889634

F32 = jnp.float32
BF16 = jnp.bfloat16


def dot(left, right):
    return jnp.dot(left, right, preferred_element_type=F32)


def dot_rows(left, right):
    return lax.dot_general(left, right, (((1,), (1,)), ((), ())), preferred_element_type=F32)


def layer_norm(values):
    average = jnp.mean(values, axis=-1, keepdims=True)
    centred = values - average
    variance = jnp.mean(centred * centred, axis=-1, keepdims=True)
    return centred * lax.rsqrt(variance + 1e-06)


def iota(shape, dim):
    return lax.broadcasted_iota(jnp.int32, shape, dim)


def head_gather():
    feature, column = iota((WIDTH, LANES), 0), iota((WIDTH, LANES), 1)
    head = jnp.where(column >= HEADS, column - HEADS, column)
    start = head * HEAD_FEATURES
    inside = (feature >= start) & (feature < start + HEAD_FEATURES) & (column < 2 * HEADS)
    return jnp.where(inside, 1.0, 0.0).astype(BF16)


def head_spread():
    column, feature = iota((LANES, WIDTH), 0), iota((LANES, WIDTH), 1)
    head = jnp.where(column >= HEADS, column - HEADS, column)
    start = head * HEAD_FEATURES
    inside = (feature >= start) & (feature < start + HEAD_FEATURES) & (column < 2 * HEADS)
    return jnp.where(inside, 1.0, 0.0).astype(BF16)


def head_norm(packed, gather, spread, scale):
    values = packed.astype(F32)
    squares = dot((values * values).astype(BF16), gather) * (1.0 / HEAD_FEATURES)
    factor = lax.rsqrt(squares + 1e-06) * scale
    high = factor.astype(BF16)
    low = (factor - high.astype(F32)).astype(BF16)
    column = iota(factor.shape, 1)
    both = jnp.where(column < HEADS, high.astype(F32), jnp.where(column < 2 * HEADS, low.astype(F32), 0.0))
    return (values * dot(both.astype(BF16), spread)).astype(BF16)


def block_table(picks):
    blocks = picks.shape[1]
    row = iota((blocks, blocks), 0)
    hits = row == picks[0:1]
    for pick in range(1, picks.shape[0]):
        hits = hits | (row == picks[pick : pick + 1])
    return jnp.where(hits, 1.0, 0.0)


def block_mask(table, query_block, key_block):
    blocks = table.shape[0]
    queries, keys = query_block.shape[0], key_block.shape[0]
    query_hot = jnp.where(query_block == iota((queries, blocks), 1), 1.0, 0.0)
    key_hot = jnp.where(key_block == iota((keys, blocks), 1), 1.0, 0.0)
    return dot_rows(dot_rows(query_hot, table), key_hot)


def shift_of(size):
    assert size & (size - 1) == 0
    return size.bit_length() - 1


def head_window(head):
    first = head * HEAD_FEATURES
    tile = first // LANES
    width = LANES if (first + HEAD_FEATURES - 1) // LANES == tile else 2 * LANES
    return tile * LANES, width, first - tile * LANES


def attend(query_of, key_of, value_of, mask, store):
    for head in range(HEADS):
        start, width, offset = head_window(head)
        window = slice(start, start + width)
        keys, values = key_of(window), value_of(window)
        lane = iota((1, width), 1)
        inside = (lane >= offset) & (lane < offset + HEAD_FEATURES)
        spare = 0 if offset > 0 else HEAD_FEATURES
        marks = jnp.where(inside, 1.0, 0.0).astype(BF16)
        ones = jnp.where(lane == spare, 1.0, 0.0).astype(BF16)
        scores = dot_rows(query_of(window), keys * marks)
        weights = jnp.exp2(scores).astype(BF16) * mask
        blended = dot(weights, values * marks + ones)
        blended = blended * (1.0 / blended[:, spare : spare + 1])
        store(window, inside, blended.astype(BF16))


def merge(ref, row, window, inside, blended):
    old = ref[row, window]
    ref[row, window] = jnp.where(jnp.broadcast_to(inside, blended.shape), blended, old)


def lay_shards(refs, near, column, weight, sem):
    me = lax.axis_index("dp")
    rows, width = refs[0].shape[0], weight.shape[1]
    copies = []
    for k, ref in enumerate(refs):
        place = weight.at[pl.ds(pl.multiple_of(jnp.bitwise_xor(me, k) * rows, 16), rows), :]
        if k < near:
            source = ref if ref.shape[1] == width else ref.at[:, pl.ds(column, width)]
            copies.append(pltpu.make_async_copy(source, place, sem.at[k]))
            copies[-1].start()
        else:
            place[...] = ref[...]
    return copies


def wait_all(copies):
    for copy in copies:
        copy.wait()


def norm_kernel(x_ref, out_ref, near_ref, far_ref, token_ref):
    normed = layer_norm(x_ref[...].astype(F32)).astype(BF16)
    out_ref[...] = normed
    half = WIDTH // 2
    pair = (lax.axis_index("dp") >> 1) & 1

    @pl.when(pair == 0)
    def _():
        near_ref[...] = normed[:, :half]
        far_ref[...] = normed[:, half:]

    @pl.when(pair == 1)
    def _():
        near_ref[...] = normed[:, half:]
        far_ref[...] = normed[:, :half]

    token_ref[...] = jnp.zeros_like(token_ref)


def half_place(k, rows, weight):
    place = jnp.bitwise_xor(lax.axis_index("dp"), k) & 1
    return weight.at[pl.ds(pl.multiple_of(place * rows, 16), rows), :]


def space_near_kernel(near_ref, own_ref, mate_ref, _, second_ref, v_ref, token_ref, weight, v_weight, sem):
    rows = own_ref.shape[0]
    column = pl.multiple_of((1 - (lax.axis_index("tm") & 1)) * WIDTH, LANES)

    @pl.when(pl.program_id(0) == 0)
    def _():
        copies = []
        for k, ref in enumerate((own_ref, mate_ref)):
            for i, (first, into) in enumerate(((2 * WIDTH, v_weight), (column, weight))):
                source = ref.at[:, pl.ds(first, WIDTH)]
                copies.append(pltpu.make_async_copy(source, half_place(k, rows, into), sem.at[k, i]))
                copies[-1].start()
        wait_all(copies)
        token_ref[...] = jnp.zeros_like(token_ref)

    near = near_ref[...]
    v_ref[...] = dot(near, v_weight[...])
    second_ref[...] = dot(near, weight[...])


def part_scale(part):
    return jnp.where(part == 0, QUERY_SCALE, 1.0).astype(F32)


def space_first_kernel(n, normed_ref, *refs):
    w_refs, (_, out_ref, token_ref, weight, sem) = refs[:n], refs[n:]
    part = lax.axis_index("tm") & 1

    @pl.when(pl.program_id(0) == 0)
    def _():
        wait_all(lay_shards(w_refs, NEAR, pl.multiple_of(part * WIDTH, LANES), weight, sem))
        token_ref[...] = jnp.zeros_like(token_ref)

    packed = dot(normed_ref[...], weight[...]).astype(BF16)
    out_ref[...] = head_norm(packed, head_gather(), head_spread(), part_scale(part))


def pick_queries(part, first_ref, second_ref, queries, q_s, k_s):
    @pl.when(part == 0)
    def _():
        q_s[...] = first_ref[queries, :]
        k_s[...] = second_ref[...]

    @pl.when(part == 1)
    def _():
        q_s[...] = second_ref[queries, :]
        k_s[...] = first_ref[...]


def space_blocks(first_row, picks, v_ref, out_ref, q_s, k_s):
    rows, patches = q_s.shape[0], k_s.shape[0]
    shift = shift_of(patches // picks.shape[1])
    query_block = (iota((rows, 1), 0) + first_row) >> shift
    key_block = iota((patches, 1), 0) >> shift
    mask = block_mask(block_table(picks), query_block, key_block).astype(BF16)
    attend(
        lambda window: q_s[:, window],
        lambda window: k_s[:, window],
        lambda window: v_ref[:, window],
        mask,
        lambda window, inside, blended: merge(out_ref, slice(0, rows), window, inside, blended),
    )


def space_rest_kernel(far_ref, first_ref, second_near, v_near, picks_ref, *refs):
    (second_there, second_mate, v_there, v_mate), refs = refs[:4], refs[4:]
    _, second_ref, v_ref, out_ref, token_ref, weight, v_weight, q_s, k_s = refs
    part = lax.axis_index("tm") & 1

    @pl.when(pl.program_id(0) == 0)
    def _():
        for k, (second, values) in enumerate(((second_there, v_there), (second_mate, v_mate))):
            half_place(k, second.shape[0], weight)[...] = second[...]
            half_place(k, values.shape[0], v_weight)[...] = values[...]
        token_ref[...] = jnp.zeros_like(token_ref)

    far = far_ref[...]
    v_ref[...] = (v_near[...] + dot(far, v_weight[...])).astype(BF16)
    packed = (second_near[...] + dot(far, weight[...])).astype(BF16)
    second_ref[...] = head_norm(packed, head_gather(), head_spread(), part_scale(1 - part))
    pick_queries(part, first_ref, second_ref, pl.ds(0, q_s.shape[0]), q_s, k_s)
    space_blocks(0, picks_ref[...], v_ref, out_ref, q_s, k_s)


def space_attend_kernel(first_row, first_ref, second_ref, v_ref, picks_ref, _, out_ref, q_s, k_s):
    part = lax.axis_index("tm") & 1
    pick_queries(part, first_ref, second_ref, pl.ds(first_row, q_s.shape[0]), q_s, k_s)
    space_blocks(first_row, picks_ref[...], v_ref, out_ref, q_s, k_s)


def space_out_kernel(n, attended_ref, x_ref, *refs):
    w_refs, (hidden_ref, token_ref, weight, sem) = refs[:n], refs[n:]

    @pl.when(pl.program_id(0) == 0)
    def _():
        wait_all(lay_shards(w_refs, NEAR, 0, weight, sem))
        token_ref[...] = jnp.zeros_like(token_ref)

    branch = dot(attended_ref[...], weight[...])
    hidden = (x_ref[...].astype(F32) + branch).astype(BF16)
    hidden_ref[...] = hidden.reshape(hidden_ref.shape)


def time_qk_kernel(n, x_ref, *refs):
    w_refs, (_, q_ref, k_ref, token_ref, weight, sem) = refs[:n], refs[n:]
    token_ref[...] = jnp.zeros_like(token_ref)
    copies = [lay_shards(w_refs, n, part * WIDTH, weight.at[part], sem.at[part]) for part in range(2)]
    gather, spread = head_gather(), head_spread()
    normed = layer_norm(x_ref[...].astype(F32)).astype(BF16)
    wait_all(copies[0])
    q_ref[...] = head_norm(dot(normed, weight[0]).astype(BF16), gather, spread, QUERY_SCALE)
    wait_all(copies[1])
    k_ref[...] = head_norm(dot(normed, weight[1]).astype(BF16), gather, spread, 1.0)


def time_kernel(n, patches_here, x_ref, picks_ref, q_s, k_s, *refs):
    w_refs, (_, attended, token_ref, weight, v_s, sem) = refs[:n], refs[n:]
    token_ref[...] = jnp.zeros_like(token_ref)
    copies = lay_shards(w_refs, n, 2 * WIDTH, weight, sem)
    rows = x_ref.shape[0]
    frames = rows // patches_here
    tile_patches = 16 if patches_here % 16 == 0 else patches_here
    tile = tile_patches * frames
    pattern = picks_ref[...]
    shift = shift_of(tile_patches)
    block_shift = shift_of(frames // pattern.shape[1]) + shift
    block = iota((tile, 1), 0) >> block_shift
    allowed = block_mask(block_table(pattern), block, block)
    same = (iota((tile, tile), 0) & (tile_patches - 1)) == (iota((tile, tile), 1) & (tile_patches - 1))
    mask = jnp.where(same, allowed, 0.0).astype(BF16)
    normed = layer_norm(x_ref[...].astype(F32)).astype(BF16)
    wait_all(copies)
    v_s[...] = dot(normed, weight[...]).astype(BF16)

    for first in range(0, patches_here, tile_patches):

        def rows_of(ref, window):
            if tile_patches == patches_here:
                return ref[:, window]
            return jnp.concatenate(
                [ref[pl.ds(f * patches_here + first, tile_patches), window] for f in range(frames)], axis=0
            )

        def store(window, inside, blended):
            if tile_patches == patches_here:
                merge(attended, slice(0, rows), window, inside, blended)
                return
            for f in range(frames):
                merge(
                    attended,
                    pl.ds(f * patches_here + first, tile_patches),
                    window,
                    inside,
                    blended[f * tile_patches : (f + 1) * tile_patches],
                )

        attend(
            partial(rows_of, q_s), partial(rows_of, k_s), partial(rows_of, v_s), mask, store
        )


def time_out_kernel(n, attended_ref, x_ref, *refs):
    w_refs, (_, out_ref, token_ref, weight, sem) = refs[:n], refs[n:]
    wait_all(lay_shards(w_refs, NEAR, 0, weight, sem))
    token_ref[...] = jnp.zeros_like(token_ref)
    out_ref[...] = (x_ref[...].astype(F32) + dot(attended_ref[...], weight[...])).astype(BF16)


HBM = pl.BlockSpec(memory_space=pl.ANY)
WHOLE = pl.BlockSpec(memory_space=pltpu.VMEM)
TOKEN = jax.ShapeDtypeStruct((8, LANES), F32)
TOKEN_SPEC = pl.BlockSpec((8, LANES), lambda *_: (0, 0))


def params(mib):
    return pltpu.CompilerParams(vmem_limit_bytes=mib * MIB)


def cost(rows, depth, columns, extra=0):
    return pl.CostEstimate(flops=rows * depth * columns // 8, bytes_accessed=2 * rows * columns // 8, transcendentals=0)


def norm_rows(rows_in):
    rows, step = rows_in.shape[0], 256
    spec = pl.BlockSpec((step, WIDTH), lambda i: (i, 0))
    half = pl.BlockSpec((step, WIDTH // 2), lambda i: (i, 0))
    return pl.pallas_call(
        norm_kernel,
        grid=(rows // step,),
        in_specs=[spec],
        out_specs=[spec, half, half, TOKEN_SPEC],
        out_shape=[jax.ShapeDtypeStruct((rows, WIDTH), BF16)]
        + [jax.ShapeDtypeStruct((rows, WIDTH // 2), BF16)] * 2
        + [TOKEN],
        compiler_params=params(12),
        name="norm_rows",
    )(rows_in)


def space_near(near, own, own_mate, token):
    rows, step = near.shape[0], 256
    flat = pl.BlockSpec((step, WIDTH), lambda i: (i, 0))
    return pl.pallas_call(
        space_near_kernel,
        grid=(rows // step,),
        in_specs=[pl.BlockSpec((step, WIDTH // 2), lambda i: (i, 0)), HBM, HBM, HBM],
        out_specs=[flat, flat, TOKEN_SPEC],
        out_shape=[jax.ShapeDtypeStruct((rows, WIDTH), F32)] * 2 + [TOKEN],
        scratch_shapes=[pltpu.VMEM((WIDTH // 2, WIDTH), BF16)] * 2 + [pltpu.SemaphoreType.DMA((2, 2))],
        compiler_params=params(14),
        cost_estimate=cost(rows, WIDTH, WIDTH),
        name="space_near",
    )(near, own, own_mate, token)


def shard_specs(n):
    return [HBM] * NEAR + [WHOLE] * (n - NEAR)


def space_first(normed, shards_of, token):
    rows, n, step = normed.shape[0], len(shards_of), 256
    flat = pl.BlockSpec((step, WIDTH), lambda i: (i, 0))
    return pl.pallas_call(
        partial(space_first_kernel, n),
        grid=(rows // step,),
        in_specs=[flat] + shard_specs(n) + [HBM],
        out_specs=[flat, TOKEN_SPEC],
        out_shape=[jax.ShapeDtypeStruct((rows, WIDTH), BF16), TOKEN],
        scratch_shapes=[pltpu.VMEM((WIDTH, WIDTH), BF16), pltpu.SemaphoreType.DMA((NEAR,))],
        compiler_params=params(14),
        cost_estimate=cost(rows, WIDTH, WIDTH),
        name="space_first",
    )(normed, *shards_of, token)


def space_rest(frames, far, first, second_near, v_near, second_shards, v_shards, picks, token):
    patches = far.shape[0] // frames
    rows = patches // CHUNKS
    frame = pl.BlockSpec((patches, WIDTH), lambda f: (f, 0))
    return pl.pallas_call(
        space_rest_kernel,
        grid=(frames,),
        in_specs=[pl.BlockSpec((patches, WIDTH // 2), lambda f: (f, 0)), frame, frame, frame] + [WHOLE] * 5 + [HBM],
        out_specs=[frame, frame, pl.BlockSpec((None, rows, WIDTH), lambda f: (f, 0, 0)), TOKEN_SPEC],
        out_shape=[jax.ShapeDtypeStruct(first.shape, BF16)] * 2
        + [jax.ShapeDtypeStruct((frames, rows, WIDTH), BF16), TOKEN],
        scratch_shapes=[pltpu.VMEM((WIDTH // 2, WIDTH), BF16)] * 2
        + [pltpu.VMEM((rows, WIDTH), BF16), pltpu.VMEM((patches, WIDTH), BF16)],
        compiler_params=params(32),
        cost_estimate=cost(frames * patches, WIDTH, 2 * WIDTH),
        name="space_rest",
    )(far, first, second_near, v_near, picks, *second_shards, *v_shards, token)


def space_attend(chunk, frames, first, second, v, picks, token):
    patches = v.shape[0] // frames
    rows = patches // CHUNKS
    frame = pl.BlockSpec((patches, WIDTH), lambda f: (f, 0))
    return pl.pallas_call(
        partial(space_attend_kernel, chunk * rows),
        grid=(frames,),
        in_specs=[frame, frame, frame, WHOLE, HBM],
        out_specs=pl.BlockSpec((None, rows, WIDTH), lambda f: (f, 0, 0)),
        out_shape=jax.ShapeDtypeStruct((frames, rows, WIDTH), BF16),
        scratch_shapes=[pltpu.VMEM((rows, WIDTH), BF16), pltpu.VMEM((patches, WIDTH), BF16)],
        compiler_params=params(18),
        cost_estimate=cost(frames * rows, WIDTH, WIDTH),
        name=f"space_attend_{chunk}",
    )(first, second, v, picks, token)


def space_out(chunk, peers, attended, clips, shards_of):
    frames, rows, n = attended.shape[0], attended.shape[1], len(shards_of)
    each = rows // peers
    direct = each % 16 == 0
    if direct:
        out_spec = pl.BlockSpec((peers, 1, each, WIDTH), lambda f: (0, f, 0, 0))
        shape = (peers, frames, each, WIDTH)
    else:
        out_spec = pl.BlockSpec((None, rows, WIDTH), lambda f: (f, 0, 0))
        shape = (frames, rows, WIDTH)
    hidden, token = pl.pallas_call(
        partial(space_out_kernel, n),
        grid=(frames,),
        in_specs=[
            pl.BlockSpec((None, rows, WIDTH), lambda f: (f, 0, 0)),
            pl.BlockSpec((None, rows, WIDTH), lambda f: (f, chunk, 0)),
        ]
        + shard_specs(n),
        out_specs=[out_spec, TOKEN_SPEC],
        out_shape=[jax.ShapeDtypeStruct(shape, BF16), TOKEN],
        scratch_shapes=[pltpu.VMEM((WIDTH, WIDTH), BF16), pltpu.SemaphoreType.DMA((NEAR,))],
        compiler_params=params(12),
        cost_estimate=cost(frames * rows, WIDTH, WIDTH),
        name=f"space_out_{chunk}",
    )(attended, clips, *shards_of)
    if not direct:
        hidden = jnp.swapaxes(hidden.reshape(frames, peers, each, WIDTH), 0, 1)
    return hidden, token


def time_qk(chunk, moved, shards_of, token):
    rows, n = moved.shape[0], len(shards_of)
    return pl.pallas_call(
        partial(time_qk_kernel, n),
        in_specs=[WHOLE] + [HBM] * (n + 1),
        out_specs=[WHOLE] * 3,
        out_shape=[jax.ShapeDtypeStruct((rows, WIDTH), BF16)] * 2 + [TOKEN],
        scratch_shapes=[pltpu.VMEM((2, WIDTH, WIDTH), BF16), pltpu.SemaphoreType.DMA((2, n))],
        compiler_params=params(30),
        cost_estimate=cost(rows, WIDTH, 2 * WIDTH),
        name=f"time_qk_{chunk}",
    )(moved, *shards_of, token)


def time_attend(chunk, moved, patches_here, picks, queries, keys, shards_of, token):
    rows, n = moved.shape[0], len(shards_of)
    return pl.pallas_call(
        partial(time_kernel, n, patches_here),
        in_specs=[WHOLE] * 4 + [HBM] * (n + 1),
        out_specs=[WHOLE, WHOLE],
        out_shape=[jax.ShapeDtypeStruct((rows, WIDTH), BF16), TOKEN],
        scratch_shapes=[
            pltpu.VMEM((WIDTH, WIDTH), BF16),
            pltpu.VMEM((rows, WIDTH), BF16),
            pltpu.SemaphoreType.DMA((n,)),
        ],
        compiler_params=params(30),
        cost_estimate=cost(rows, WIDTH, 2 * WIDTH),
        name=f"time_attend_{chunk}",
    )(moved, picks, queries, keys, *shards_of, token)


def time_out(chunk, attended, moved, shards_of, token):
    rows, n = moved.shape[0], len(shards_of)
    return pl.pallas_call(
        partial(time_out_kernel, n),
        in_specs=[WHOLE, WHOLE] + shard_specs(n) + [HBM],
        out_specs=[WHOLE, WHOLE],
        out_shape=[jax.ShapeDtypeStruct((rows, WIDTH), BF16), TOKEN],
        scratch_shapes=[pltpu.VMEM((WIDTH, WIDTH), BF16), pltpu.SemaphoreType.DMA((NEAR,))],
        compiler_params=params(16),
        cost_estimate=cost(rows, WIDTH, WIDTH),
        name=f"time_out_{chunk}",
    )(attended, moved, *shards_of, token)


def place_kernel(back_ref, *refs):
    out_ref = refs[-1]
    out_ref[...] = back_ref[...].reshape(out_ref.shape)


def place(chunk, back, patches, into):
    peers, frames, each, _ = back.shape
    rows = peers * each
    return pl.pallas_call(
        place_kernel,
        grid=(frames,),
        in_specs=[pl.BlockSpec((peers, None, each, WIDTH), lambda f: (0, f, 0, 0))] + [HBM] * len(into),
        out_specs=pl.BlockSpec((None, rows, WIDTH), lambda f: (f, chunk, 0)),
        out_shape=jax.ShapeDtypeStruct((frames, patches, WIDTH), BF16),
        input_output_aliases={1: 0} if into else {},
        compiler_params=params(8),
        name=f"place_{chunk}",
    )(back, *into)


def swap(value, mask, axis="dp"):
    return lax.ppermute(value, axis, [(i, i ^ mask) for i in range(lax.axis_size(axis))])


def after(value, other):
    return pl.pallas_call(
        lambda *refs: None,
        in_specs=[HBM] * 2,
        out_specs=HBM,
        out_shape=jax.ShapeDtypeStruct(value.shape, value.dtype),
        input_output_aliases={0: 0},
        compiler_params=params(1),
        name="after",
    )(value, other)


def split_kernel(w_ref, _, qk_ref, v_ref, token_ref):
    qk_ref[...] = w_ref[:, : 2 * WIDTH]
    v_ref[...] = w_ref[:, 2 * WIDTH :]
    token_ref[...] = jnp.zeros_like(token_ref)


def split_columns(weight, token):
    rows, columns = weight.shape
    return pl.pallas_call(
        split_kernel,
        in_specs=[WHOLE, HBM],
        out_specs=[WHOLE] * 3,
        out_shape=[
            jax.ShapeDtypeStruct((rows, 2 * WIDTH), BF16),
            jax.ShapeDtypeStruct((rows, columns - 2 * WIDTH), BF16),
            TOKEN,
        ],
        compiler_params=params(8),
        name="split_columns",
    )(weight, token)


def part_kernel(w_ref, out_ref, sem):
    column = pl.multiple_of((lax.axis_index("tm") & 1) * WIDTH, LANES)
    copy = pltpu.make_async_copy(w_ref.at[:, pl.ds(column, WIDTH)], out_ref, sem)
    copy.start()
    copy.wait()


def part_columns(weight):
    return pl.pallas_call(
        part_kernel,
        in_specs=[HBM],
        out_specs=WHOLE,
        out_shape=jax.ShapeDtypeStruct((weight.shape[0], WIDTH), BF16),
        scratch_shapes=[pltpu.SemaphoreType.DMA],
        compiler_params=params(4),
        name="part_columns",
    )(weight)


def held(value, token):
    probe = token[0, 0]
    return jnp.where(probe != probe, jnp.zeros_like(value), value)


def together(*values):
    n = len(values)
    return pl.pallas_call(
        lambda *refs: None,
        in_specs=[HBM] * n,
        out_specs=[HBM] * n,
        out_shape=[jax.ShapeDtypeStruct(value.shape, value.dtype) for value in values],
        input_output_aliases={i: i for i in range(n)},
        compiler_params=params(1),
        name="together",
    )(*values)


def shards(clips, w_space_qkv, w_space_out, w_time_qkv, w_time_out, space_pattern, time_pattern):
    peers = lax.axis_size("tm")
    frames, patches = clips.shape[1], clips.shape[2]
    frames_all = frames * peers
    each = patches // CHUNKS // peers
    local = clips.reshape(frames, patches, WIDTH)
    space_picks, time_picks = space_pattern.T, time_pattern.T

    first_there = swap(part_columns(w_space_qkv), 2)
    own_mate = swap(w_space_qkv, 1)
    own = [w_space_qkv, own_mate]
    normed, near, far, token = norm_rows(local.reshape(frames * patches, WIDTH))
    second_near, v_near, token = space_near(near, w_space_qkv, own_mate, token)
    time_qk_own, time_v_own, token = split_columns(w_time_qkv, token)
    first_there, token = together(first_there, token)
    first_mate = swap(first_there, 1)
    second_there = swap(first_there, 1, "tm")
    v_there = swap(w_space_qkv[:, 2 * WIDTH :], 2)
    out_there = swap(w_space_out, 2)
    (token,) = together(token)
    first, token = space_first(normed, own + [first_there, first_mate], token)
    second_there, v_there, token = together(second_there, v_there, token)
    second_mate, v_mate = swap(second_there, 1), swap(v_there, 1)
    (token,) = together(token)
    second, v, attended, token = space_rest(
        frames, far, first, second_near, v_near, [second_there, second_mate], [v_there, v_mate], space_picks, token
    )
    out_there, token = together(out_there, token)
    space_out_shards = [w_space_out, swap(w_space_out, 1), out_there, swap(out_there, 1)]
    moved = []
    for chunk in range(CHUNKS):
        if chunk > 0:
            attended = space_attend(chunk, frames, first, second, v, space_picks, token)
        hidden, token = space_out(chunk, peers, attended, local, space_out_shards)
        moved.append(lax.all_to_all(hidden, "tm", split_axis=0, concat_axis=0, tiled=True))
    qk_there, time_v_there = swap(time_qk_own, 2), swap(time_v_own, 2)
    qk_there, token = together(qk_there, token)
    time_mate = swap(w_time_qkv, 1)
    qk_shards = [w_time_qkv, time_mate, qk_there, swap(qk_there, 1)]
    time_there = swap(w_time_out, 2)
    returned = []
    for chunk in range(CHUNKS):
        rows = moved[chunk].reshape(frames_all * each, WIDTH)
        queries, keys, token = time_qk(chunk, rows, qk_shards, token)
        if chunk == 0:
            time_v_there = held(time_v_there, token)
            v_shards = [w_time_qkv, time_mate, time_v_there, swap(time_v_there, 1)]
            time_there = held(time_there, token)
            time_shards = [w_time_out, swap(w_time_out, 1), time_there, swap(time_there, 1)]
        attended, token = time_attend(chunk, rows, each, time_picks, queries, keys, v_shards, token)
        finished, token = time_out(chunk, attended, rows, time_shards, token)
        finished = finished.reshape(peers, frames, each, WIDTH)
        if chunk > 0:
            finished = after(finished, back)
        back = lax.all_to_all(finished, "tm", split_axis=0, concat_axis=0, tiled=True)
        if each % 16 == 0:
            returned = [place(chunk, back, patches, returned)]
        else:
            returned.append(jnp.swapaxes(back, 0, 1).reshape(frames, patches // CHUNKS, WIDTH))
    return (returned[0] if len(returned) == 1 else jnp.concatenate(returned, axis=1))[None]


def solution(mesh):
    return jax.shard_map(
        shards,
        mesh=mesh,
        in_specs=(
            P("dp", "tm", None, None),
            P("dp", None),
            P("dp", None),
            P("dp", None),
            P("dp", None),
            P(),
            P(),
        ),
        out_specs=P("dp", "tm", None, None),
        check_vma=False,
    )
```

```python
from functools import partial

import jax
import jax.numpy as jnp
from jax import lax
from jax.experimental import pallas as pl
from jax.experimental.pallas import tpu as pltpu
from jax.sharding import PartitionSpec as P

HEADS = 16
HEAD_FEATURES = 72
WIDTH = 1152
CHUNKS = 2
NEAR = 2
LANES = 128
MIB = 1024 * 1024
QUERY_SCALE = HEAD_FEATURES**-0.5 * 1.4426950408889634

F32 = jnp.float32
BF16 = jnp.bfloat16


def dot(left, right):
    return jnp.dot(left, right, preferred_element_type=F32)


def dot_rows(left, right):
    return lax.dot_general(left, right, (((1,), (1,)), ((), ())), preferred_element_type=F32)


def layer_norm(values):
    average = jnp.mean(values, axis=-1, keepdims=True)
    centred = values - average
    variance = jnp.mean(centred * centred, axis=-1, keepdims=True)
    return centred * lax.rsqrt(variance + 1e-06)


def iota(shape, dim):
    return lax.broadcasted_iota(jnp.int32, shape, dim)


def head_gather():
    feature, column = iota((WIDTH, LANES), 0), iota((WIDTH, LANES), 1)
    head = jnp.where(column >= HEADS, column - HEADS, column)
    start = head * HEAD_FEATURES
    inside = (feature >= start) & (feature < start + HEAD_FEATURES) & (column < 2 * HEADS)
    return jnp.where(inside, 1.0, 0.0).astype(BF16)


def head_spread():
    column, feature = iota((LANES, WIDTH), 0), iota((LANES, WIDTH), 1)
    head = jnp.where(column >= HEADS, column - HEADS, column)
    start = head * HEAD_FEATURES
    inside = (feature >= start) & (feature < start + HEAD_FEATURES) & (column < 2 * HEADS)
    return jnp.where(inside, 1.0, 0.0).astype(BF16)


def head_norm(packed, gather, spread, scale):
    values = packed.astype(F32)
    squares = dot((values * values).astype(BF16), gather) * (1.0 / HEAD_FEATURES)
    factor = lax.rsqrt(squares + 1e-06) * scale
    high = factor.astype(BF16)
    low = (factor - high.astype(F32)).astype(BF16)
    column = iota(factor.shape, 1)
    both = jnp.where(column < HEADS, high.astype(F32), jnp.where(column < 2 * HEADS, low.astype(F32), 0.0))
    return (values * dot(both.astype(BF16), spread)).astype(BF16)


def block_table(picks):
    blocks = picks.shape[1]
    row = iota((blocks, blocks), 0)
    hits = row == picks[0:1]
    for pick in range(1, picks.shape[0]):
        hits = hits | (row == picks[pick : pick + 1])
    return jnp.where(hits, 1.0, 0.0)


def block_mask(table, query_block, key_block):
    blocks = table.shape[0]
    queries, keys = query_block.shape[0], key_block.shape[0]
    query_hot = jnp.where(query_block == iota((queries, blocks), 1), 1.0, 0.0)
    key_hot = jnp.where(key_block == iota((keys, blocks), 1), 1.0, 0.0)
    return dot_rows(dot_rows(query_hot, table), key_hot)


def shift_of(size):
    assert size & (size - 1) == 0
    return size.bit_length() - 1


def head_window(head):
    first = head * HEAD_FEATURES
    tile = first // LANES
    width = LANES if (first + HEAD_FEATURES - 1) // LANES == tile else 2 * LANES
    return tile * LANES, width, first - tile * LANES


def attend(query_of, key_of, value_of, mask, store):
    for head in range(HEADS):
        start, width, offset = head_window(head)
        window = slice(start, start + width)
        keys, values = key_of(window), value_of(window)
        lane = iota((1, width), 1)
        inside = (lane >= offset) & (lane < offset + HEAD_FEATURES)
        spare = 0 if offset > 0 else HEAD_FEATURES
        marks = jnp.where(inside, 1.0, 0.0).astype(BF16)
        ones = jnp.where(lane == spare, 1.0, 0.0).astype(BF16)
        scores = dot_rows(query_of(window), keys * marks)
        weights = jnp.exp2(scores).astype(BF16) * mask
        blended = dot(weights, values * marks + ones)
        blended = blended * (1.0 / blended[:, spare : spare + 1])
        store(window, inside, blended.astype(BF16))


def merge(ref, row, window, inside, blended):
    old = ref[row, window]
    ref[row, window] = jnp.where(jnp.broadcast_to(inside, blended.shape), blended, old)


def lay_shards(refs, near, column, weight, sem):
    me = lax.axis_index("dp")
    rows, width = refs[0].shape[0], weight.shape[1]
    copies = []
    for k, ref in enumerate(refs):
        place = weight.at[pl.ds(pl.multiple_of(jnp.bitwise_xor(me, k) * rows, 16), rows), :]
        if k < near:
            source = ref if ref.shape[1] == width else ref.at[:, pl.ds(column, width)]
            copies.append(pltpu.make_async_copy(source, place, sem.at[k]))
            copies[-1].start()
        else:
            place[...] = ref[...]
    return copies


def wait_all(copies):
    for copy in copies:
        copy.wait()


def norm_kernel(x_ref, out_ref, near_ref, far_ref, token_ref):
    normed = layer_norm(x_ref[...].astype(F32)).astype(BF16)
    out_ref[...] = normed
    half = WIDTH // 2
    pair = (lax.axis_index("dp") >> 1) & 1

    @pl.when(pair == 0)
    def _():
        near_ref[...] = normed[:, :half]
        far_ref[...] = normed[:, half:]

    @pl.when(pair == 1)
    def _():
        near_ref[...] = normed[:, half:]
        far_ref[...] = normed[:, :half]

    token_ref[...] = jnp.zeros_like(token_ref)


def half_place(k, rows, weight):
    place = jnp.bitwise_xor(lax.axis_index("dp"), k) & 1
    return weight.at[pl.ds(pl.multiple_of(place * rows, 16), rows), :]


def space_near_kernel(near_ref, own_ref, mate_ref, _, second_ref, v_ref, token_ref, weight, v_weight, sem):
    rows = own_ref.shape[0]
    column = pl.multiple_of((1 - (lax.axis_index("tm") & 1)) * WIDTH, LANES)

    @pl.when(pl.program_id(0) == 0)
    def _():
        copies = []
        for k, ref in enumerate((own_ref, mate_ref)):
            for i, (first, into) in enumerate(((2 * WIDTH, v_weight), (column, weight))):
                source = ref.at[:, pl.ds(first, WIDTH)]
                copies.append(pltpu.make_async_copy(source, half_place(k, rows, into), sem.at[k, i]))
                copies[-1].start()
        wait_all(copies)
        token_ref[...] = jnp.zeros_like(token_ref)

    near = near_ref[...]
    v_ref[...] = dot(near, v_weight[...])
    second_ref[...] = dot(near, weight[...])


def part_scale(part):
    return jnp.where(part == 0, QUERY_SCALE, 1.0).astype(F32)


def space_first_kernel(n, normed_ref, *refs):
    w_refs, (_, out_ref, token_ref, weight, sem) = refs[:n], refs[n:]
    part = lax.axis_index("tm") & 1

    @pl.when(pl.program_id(0) == 0)
    def _():
        wait_all(lay_shards(w_refs, NEAR, pl.multiple_of(part * WIDTH, LANES), weight, sem))
        token_ref[...] = jnp.zeros_like(token_ref)

    packed = dot(normed_ref[...], weight[...]).astype(BF16)
    out_ref[...] = head_norm(packed, head_gather(), head_spread(), part_scale(part))


def pick_queries(part, first_ref, second_ref, queries, q_s, k_s):
    @pl.when(part == 0)
    def _():
        q_s[...] = first_ref[queries, :]
        k_s[...] = second_ref[...]

    @pl.when(part == 1)
    def _():
        q_s[...] = second_ref[queries, :]
        k_s[...] = first_ref[...]


def space_blocks(first_row, picks, v_ref, out_ref, q_s, k_s):
    rows, patches = q_s.shape[0], k_s.shape[0]
    shift = shift_of(patches // picks.shape[1])
    query_block = (iota((rows, 1), 0) + first_row) >> shift
    key_block = iota((patches, 1), 0) >> shift
    mask = block_mask(block_table(picks), query_block, key_block).astype(BF16)
    attend(
        lambda window: q_s[:, window],
        lambda window: k_s[:, window],
        lambda window: v_ref[:, window],
        mask,
        lambda window, inside, blended: merge(out_ref, slice(0, rows), window, inside, blended),
    )


def space_rest_kernel(far_ref, first_ref, second_near, v_near, picks_ref, *refs):
    (second_there, second_mate, v_there, v_mate), refs = refs[:4], refs[4:]
    _, second_ref, v_ref, out_ref, token_ref, weight, v_weight, q_s, k_s = refs
    part = lax.axis_index("tm") & 1

    @pl.when(pl.program_id(0) == 0)
    def _():
        for k, (second, values) in enumerate(((second_there, v_there), (second_mate, v_mate))):
            half_place(k, second.shape[0], weight)[...] = second[...]
            half_place(k, values.shape[0], v_weight)[...] = values[...]
        token_ref[...] = jnp.zeros_like(token_ref)

    far = far_ref[...]
    v_ref[...] = (v_near[...] + dot(far, v_weight[...])).astype(BF16)
    packed = (second_near[...] + dot(far, weight[...])).astype(BF16)
    second_ref[...] = head_norm(packed, head_gather(), head_spread(), part_scale(1 - part))
    pick_queries(part, first_ref, second_ref, pl.ds(0, q_s.shape[0]), q_s, k_s)
    space_blocks(0, picks_ref[...], v_ref, out_ref, q_s, k_s)


def space_attend_kernel(first_row, first_ref, second_ref, v_ref, picks_ref, _, out_ref, q_s, k_s):
    part = lax.axis_index("tm") & 1
    pick_queries(part, first_ref, second_ref, pl.ds(first_row, q_s.shape[0]), q_s, k_s)
    space_blocks(first_row, picks_ref[...], v_ref, out_ref, q_s, k_s)


def space_out_kernel(n, attended_ref, x_ref, *refs):
    w_refs, (hidden_ref, token_ref, weight, sem) = refs[:n], refs[n:]

    @pl.when(pl.program_id(0) == 0)
    def _():
        wait_all(lay_shards(w_refs, NEAR, 0, weight, sem))
        token_ref[...] = jnp.zeros_like(token_ref)

    branch = dot(attended_ref[...], weight[...])
    hidden = (x_ref[...].astype(F32) + branch).astype(BF16)
    hidden_ref[...] = hidden.reshape(hidden_ref.shape)


def time_kernel(n, patches_here, x_ref, picks_ref, *refs):
    w_refs, (_, attended, token_ref, weight, q_s, k_s, v_s, sem) = refs[:n], refs[n:]
    token_ref[...] = jnp.zeros_like(token_ref)
    copies = [
        lay_shards(w_refs, n, part * WIDTH, weight.at[part], sem.at[part]) for part in range(3)
    ]
    rows = x_ref.shape[0]
    frames = rows // patches_here
    tile_patches = 16 if patches_here % 16 == 0 else patches_here
    tile = tile_patches * frames
    pattern = picks_ref[...]
    shift = shift_of(tile_patches)
    block_shift = shift_of(frames // pattern.shape[1]) + shift
    block = iota((tile, 1), 0) >> block_shift
    allowed = block_mask(block_table(pattern), block, block)
    same = (iota((tile, tile), 0) & (tile_patches - 1)) == (iota((tile, tile), 1) & (tile_patches - 1))
    mask = jnp.where(same, allowed, 0.0).astype(BF16)
    gather, spread = head_gather(), head_spread()
    normed = layer_norm(x_ref[...].astype(F32)).astype(BF16)
    wait_all(copies[0])
    q_s[...] = head_norm(dot(normed, weight[0]).astype(BF16), gather, spread, QUERY_SCALE)
    wait_all(copies[1])
    k_s[...] = head_norm(dot(normed, weight[1]).astype(BF16), gather, spread, 1.0)
    wait_all(copies[2])
    v_s[...] = dot(normed, weight[2]).astype(BF16)

    for first in range(0, patches_here, tile_patches):

        def rows_of(ref, window):
            if tile_patches == patches_here:
                return ref[:, window]
            return jnp.concatenate(
                [ref[pl.ds(f * patches_here + first, tile_patches), window] for f in range(frames)], axis=0
            )

        def store(window, inside, blended):
            if tile_patches == patches_here:
                merge(attended, slice(0, rows), window, inside, blended)
                return
            for f in range(frames):
                merge(
                    attended,
                    pl.ds(f * patches_here + first, tile_patches),
                    window,
                    inside,
                    blended[f * tile_patches : (f + 1) * tile_patches],
                )

        attend(
            partial(rows_of, q_s), partial(rows_of, k_s), partial(rows_of, v_s), mask, store
        )


def time_out_kernel(n, attended_ref, x_ref, *refs):
    w_refs, (_, out_ref, token_ref, weight, sem) = refs[:n], refs[n:]
    wait_all(lay_shards(w_refs, NEAR, 0, weight, sem))
    token_ref[...] = jnp.zeros_like(token_ref)
    out_ref[...] = (x_ref[...].astype(F32) + dot(attended_ref[...], weight[...])).astype(BF16)


HBM = pl.BlockSpec(memory_space=pl.ANY)
WHOLE = pl.BlockSpec(memory_space=pltpu.VMEM)
TOKEN = jax.ShapeDtypeStruct((8, LANES), F32)
TOKEN_SPEC = pl.BlockSpec((8, LANES), lambda *_: (0, 0))


def params(mib):
    return pltpu.CompilerParams(vmem_limit_bytes=mib * MIB)


def cost(rows, depth, columns, extra=0):
    return pl.CostEstimate(flops=rows * depth * columns // 8, bytes_accessed=2 * rows * columns // 8, transcendentals=0)


def norm_rows(rows_in):
    rows, step = rows_in.shape[0], 256
    spec = pl.BlockSpec((step, WIDTH), lambda i: (i, 0))
    half = pl.BlockSpec((step, WIDTH // 2), lambda i: (i, 0))
    return pl.pallas_call(
        norm_kernel,
        grid=(rows // step,),
        in_specs=[spec],
        out_specs=[spec, half, half, TOKEN_SPEC],
        out_shape=[jax.ShapeDtypeStruct((rows, WIDTH), BF16)]
        + [jax.ShapeDtypeStruct((rows, WIDTH // 2), BF16)] * 2
        + [TOKEN],
        compiler_params=params(12),
        name="norm_rows",
    )(rows_in)


def space_near(near, own, own_mate, token):
    rows, step = near.shape[0], 256
    flat = pl.BlockSpec((step, WIDTH), lambda i: (i, 0))
    return pl.pallas_call(
        space_near_kernel,
        grid=(rows // step,),
        in_specs=[pl.BlockSpec((step, WIDTH // 2), lambda i: (i, 0)), HBM, HBM, HBM],
        out_specs=[flat, flat, TOKEN_SPEC],
        out_shape=[jax.ShapeDtypeStruct((rows, WIDTH), F32)] * 2 + [TOKEN],
        scratch_shapes=[pltpu.VMEM((WIDTH // 2, WIDTH), BF16)] * 2 + [pltpu.SemaphoreType.DMA((2, 2))],
        compiler_params=params(14),
        cost_estimate=cost(rows, WIDTH, WIDTH),
        name="space_near",
    )(near, own, own_mate, token)


def shard_specs(n):
    return [HBM] * NEAR + [WHOLE] * (n - NEAR)


def space_first(normed, shards_of, token):
    rows, n, step = normed.shape[0], len(shards_of), 256
    flat = pl.BlockSpec((step, WIDTH), lambda i: (i, 0))
    return pl.pallas_call(
        partial(space_first_kernel, n),
        grid=(rows // step,),
        in_specs=[flat] + shard_specs(n) + [HBM],
        out_specs=[flat, TOKEN_SPEC],
        out_shape=[jax.ShapeDtypeStruct((rows, WIDTH), BF16), TOKEN],
        scratch_shapes=[pltpu.VMEM((WIDTH, WIDTH), BF16), pltpu.SemaphoreType.DMA((NEAR,))],
        compiler_params=params(14),
        cost_estimate=cost(rows, WIDTH, WIDTH),
        name="space_first",
    )(normed, *shards_of, token)


def space_rest(frames, far, first, second_near, v_near, second_shards, v_shards, picks, token):
    patches = far.shape[0] // frames
    rows = patches // CHUNKS
    frame = pl.BlockSpec((patches, WIDTH), lambda f: (f, 0))
    return pl.pallas_call(
        space_rest_kernel,
        grid=(frames,),
        in_specs=[pl.BlockSpec((patches, WIDTH // 2), lambda f: (f, 0)), frame, frame, frame] + [WHOLE] * 5 + [HBM],
        out_specs=[frame, frame, pl.BlockSpec((None, rows, WIDTH), lambda f: (f, 0, 0)), TOKEN_SPEC],
        out_shape=[jax.ShapeDtypeStruct(first.shape, BF16)] * 2
        + [jax.ShapeDtypeStruct((frames, rows, WIDTH), BF16), TOKEN],
        scratch_shapes=[pltpu.VMEM((WIDTH // 2, WIDTH), BF16)] * 2
        + [pltpu.VMEM((rows, WIDTH), BF16), pltpu.VMEM((patches, WIDTH), BF16)],
        compiler_params=params(32),
        cost_estimate=cost(frames * patches, WIDTH, 2 * WIDTH),
        name="space_rest",
    )(far, first, second_near, v_near, picks, *second_shards, *v_shards, token)


def space_attend(chunk, frames, first, second, v, picks, token):
    patches = v.shape[0] // frames
    rows = patches // CHUNKS
    frame = pl.BlockSpec((patches, WIDTH), lambda f: (f, 0))
    return pl.pallas_call(
        partial(space_attend_kernel, chunk * rows),
        grid=(frames,),
        in_specs=[frame, frame, frame, WHOLE, HBM],
        out_specs=pl.BlockSpec((None, rows, WIDTH), lambda f: (f, 0, 0)),
        out_shape=jax.ShapeDtypeStruct((frames, rows, WIDTH), BF16),
        scratch_shapes=[pltpu.VMEM((rows, WIDTH), BF16), pltpu.VMEM((patches, WIDTH), BF16)],
        compiler_params=params(18),
        cost_estimate=cost(frames * rows, WIDTH, WIDTH),
        name=f"space_attend_{chunk}",
    )(first, second, v, picks, token)


def space_out(chunk, peers, attended, clips, shards_of):
    frames, rows, n = attended.shape[0], attended.shape[1], len(shards_of)
    each = rows // peers
    direct = each % 16 == 0
    if direct:
        out_spec = pl.BlockSpec((peers, 1, each, WIDTH), lambda f: (0, f, 0, 0))
        shape = (peers, frames, each, WIDTH)
    else:
        out_spec = pl.BlockSpec((None, rows, WIDTH), lambda f: (f, 0, 0))
        shape = (frames, rows, WIDTH)
    hidden, token = pl.pallas_call(
        partial(space_out_kernel, n),
        grid=(frames,),
        in_specs=[
            pl.BlockSpec((None, rows, WIDTH), lambda f: (f, 0, 0)),
            pl.BlockSpec((None, rows, WIDTH), lambda f: (f, chunk, 0)),
        ]
        + shard_specs(n),
        out_specs=[out_spec, TOKEN_SPEC],
        out_shape=[jax.ShapeDtypeStruct(shape, BF16), TOKEN],
        scratch_shapes=[pltpu.VMEM((WIDTH, WIDTH), BF16), pltpu.SemaphoreType.DMA((NEAR,))],
        compiler_params=params(12),
        cost_estimate=cost(frames * rows, WIDTH, WIDTH),
        name=f"space_out_{chunk}",
    )(attended, clips, *shards_of)
    if not direct:
        hidden = jnp.swapaxes(hidden.reshape(frames, peers, each, WIDTH), 0, 1)
    return hidden, token


def time_attend(chunk, moved, patches_here, picks, shards_of, token):
    rows, n = moved.shape[0], len(shards_of)
    return pl.pallas_call(
        partial(time_kernel, n, patches_here),
        in_specs=[WHOLE, WHOLE] + [HBM] * (n + 1),
        out_specs=[WHOLE, WHOLE],
        out_shape=[jax.ShapeDtypeStruct((rows, WIDTH), BF16), TOKEN],
        scratch_shapes=[pltpu.VMEM((3, WIDTH, WIDTH), BF16)]
        + [pltpu.VMEM((rows, WIDTH), BF16)] * 3
        + [pltpu.SemaphoreType.DMA((3, n))],
        compiler_params=params(52),
        cost_estimate=cost(rows, WIDTH, 4 * WIDTH),
        name=f"time_attend_{chunk}",
    )(moved, picks, *shards_of, token)


def time_out(chunk, attended, moved, shards_of, token):
    rows, n = moved.shape[0], len(shards_of)
    return pl.pallas_call(
        partial(time_out_kernel, n),
        in_specs=[WHOLE, WHOLE] + shard_specs(n) + [HBM],
        out_specs=[WHOLE, WHOLE],
        out_shape=[jax.ShapeDtypeStruct((rows, WIDTH), BF16), TOKEN],
        scratch_shapes=[pltpu.VMEM((WIDTH, WIDTH), BF16), pltpu.SemaphoreType.DMA((NEAR,))],
        compiler_params=params(16),
        cost_estimate=cost(rows, WIDTH, WIDTH),
        name=f"time_out_{chunk}",
    )(attended, moved, *shards_of, token)


def place_kernel(back_ref, *refs):
    out_ref = refs[-1]
    out_ref[...] = back_ref[...].reshape(out_ref.shape)


def place(chunk, back, patches, into):
    peers, frames, each, _ = back.shape
    step = 2 if peers % 2 == 0 else 1
    steps, rows = peers // step, step * each
    return pl.pallas_call(
        place_kernel,
        grid=(frames, steps),
        in_specs=[pl.BlockSpec((step, None, each, WIDTH), lambda f, i: (i, f, 0, 0))] + [HBM] * len(into),
        out_specs=pl.BlockSpec((None, rows, WIDTH), lambda f, i: (f, chunk * steps + i, 0)),
        out_shape=jax.ShapeDtypeStruct((frames, patches, WIDTH), BF16),
        input_output_aliases={1: 0} if into else {},
        compiler_params=params(8),
        name=f"place_{chunk}",
    )(back, *into)


def swap(value, mask, axis="dp"):
    return lax.ppermute(value, axis, [(i, i ^ mask) for i in range(lax.axis_size(axis))])


def after(value, other):
    return pl.pallas_call(
        lambda *refs: None,
        in_specs=[HBM] * 2,
        out_specs=HBM,
        out_shape=jax.ShapeDtypeStruct(value.shape, value.dtype),
        input_output_aliases={0: 0},
        compiler_params=params(1),
        name="after",
    )(value, other)


def part_kernel(w_ref, out_ref, sem):
    column = pl.multiple_of((lax.axis_index("tm") & 1) * WIDTH, LANES)
    copy = pltpu.make_async_copy(w_ref.at[:, pl.ds(column, WIDTH)], out_ref, sem)
    copy.start()
    copy.wait()


def part_columns(weight):
    return pl.pallas_call(
        part_kernel,
        in_specs=[HBM],
        out_specs=WHOLE,
        out_shape=jax.ShapeDtypeStruct((weight.shape[0], WIDTH), BF16),
        scratch_shapes=[pltpu.SemaphoreType.DMA],
        compiler_params=params(4),
        name="part_columns",
    )(weight)


def held(value, token):
    probe = token[0, 0]
    return jnp.where(probe != probe, jnp.zeros_like(value), value)


def together(*values):
    n = len(values)
    return pl.pallas_call(
        lambda *refs: None,
        in_specs=[HBM] * n,
        out_specs=[HBM] * n,
        out_shape=[jax.ShapeDtypeStruct(value.shape, value.dtype) for value in values],
        input_output_aliases={i: i for i in range(n)},
        compiler_params=params(1),
        name="together",
    )(*values)


def shards(clips, w_space_qkv, w_space_out, w_time_qkv, w_time_out, space_pattern, time_pattern):
    peers = lax.axis_size("tm")
    frames, patches = clips.shape[1], clips.shape[2]
    frames_all = frames * peers
    each = patches // CHUNKS // peers
    local = clips.reshape(frames, patches, WIDTH)
    space_picks, time_picks = space_pattern.T, time_pattern.T

    first_there = swap(part_columns(w_space_qkv), 2)
    own_mate = swap(w_space_qkv, 1)
    own = [w_space_qkv, own_mate]
    normed, near, far, token = norm_rows(local.reshape(frames * patches, WIDTH))
    second_near, v_near, token = space_near(near, w_space_qkv, own_mate, token)
    first_there, token = together(first_there, token)
    first_mate = swap(first_there, 1)
    second_there = swap(first_there, 1, "tm")
    v_there = swap(w_space_qkv[:, 2 * WIDTH :], 2)
    out_there = swap(w_space_out, 2)
    (token,) = together(token)
    first, token = space_first(normed, own + [first_there, first_mate], token)
    second_there, v_there, token = together(second_there, v_there, token)
    second_mate, v_mate = swap(second_there, 1), swap(v_there, 1)
    (token,) = together(token)
    second, v, attended, token = space_rest(
        frames, far, first, second_near, v_near, [second_there, second_mate], [v_there, v_mate], space_picks, token
    )
    out_there, token = together(out_there, token)
    space_out_shards = [w_space_out, swap(w_space_out, 1), out_there, swap(out_there, 1)]
    moved = []
    for chunk in range(CHUNKS):
        if chunk > 0:
            attended = space_attend(chunk, frames, first, second, v, space_picks, token)
        hidden, token = space_out(chunk, peers, attended, local, space_out_shards)
        moved.append(lax.all_to_all(hidden, "tm", split_axis=0, concat_axis=0, tiled=True))
    qkv_there = swap(w_time_qkv, 2)
    qkv_there, token = together(qkv_there, token)
    time_qkv = [w_time_qkv, swap(w_time_qkv, 1), qkv_there, swap(qkv_there, 1)]
    time_there = swap(w_time_out, 2)
    returned = []
    for chunk in range(CHUNKS):
        rows = moved[chunk].reshape(frames_all * each, WIDTH)
        attended, token = time_attend(chunk, rows, each, time_picks, time_qkv, token)
        if chunk == 0:
            time_there = held(time_there, token)
            time_shards = [w_time_out, swap(w_time_out, 1), time_there, swap(time_there, 1)]
        finished, token = time_out(chunk, attended, rows, time_shards, token)
        finished = finished.reshape(peers, frames, each, WIDTH)
        if chunk > 0:
            finished = after(finished, back)
        back = lax.all_to_all(finished, "tm", split_axis=0, concat_axis=0, tiled=True)
        if each % 16 == 0:
            returned = [place(chunk, back, patches, returned)]
        else:
            returned.append(jnp.swapaxes(back, 0, 1).reshape(frames, patches // CHUNKS, WIDTH))
    return (returned[0] if len(returned) == 1 else jnp.concatenate(returned, axis=1))[None]


def solution(mesh):
    return jax.shard_map(
        shards,
        mesh=mesh,
        in_specs=(
            P("dp", "tm", None, None),
            P("dp", None),
            P("dp", None),
            P("dp", None),
            P("dp", None),
            P(),
            P(),
        ),
        out_specs=P("dp", "tm", None, None),
        check_vma=False,
    )
```
